512 devices in a mesh: gx: 8 (over z), gy: 8 (over x, core), gz: 8 (over y).
Axes of the slice: x: 4, y: 8, z: 8, core: 2. Of those that a mesh axis runs over, the one named last changes fastest.
Arguments:
- turbulence: float32 [128, 1024, 1024], P('gz', 'gx', 'gy'), may hold values from -6 to 6
Outputs:
- coefficients: float32 [128, 1024, 1024], P('gz', 'gx', 'gy')
The draws below stay inside these ranges and needn't reach their ends.
All inputs are finite; a program needn't handle non-finite values.
Results may differ from the reference program's by a relative error of at most 0.000075.
Values sent between devices are 32-bit elements; how exact they have to be, the bound alone decides.
A program may use at most 64 MiB of HBM per device.

```python
import jax
import jax.numpy as jnp
from jax import lax

NX = 1024
NY = 1024
NZ = 128
LEVELS = 3


def steps_of(stream_key, dims, pieces, least, largest):
    def one(axis_at, shards_of):
        draws = jax.random.uniform(jax.random.fold_in(jax.random.fold_in(stream_key, 6), axis_at), (shards_of,), jnp.float32, least / len(pieces), largest / len(pieces))
        return jnp.repeat(jnp.exp(draws), dims[axis_at] // shards_of).reshape((-1,) + (1,) * (len(dims) - axis_at - 1))

    gain = one(*pieces[0])
    for cut in pieces[1:]:
        gain = gain * one(*cut)
    return gain


def noise(stream_key, shape, width, bound, shards=(), dtype=jnp.bfloat16):
    gain = steps_of(stream_key, shape, shards, -0.22, 0.18) if shards else 1.0
    values = jax.random.normal(stream_key, shape, jnp.float32) * width * gain
    return jnp.minimum(jnp.maximum(values, -bound), bound).astype(dtype)


def setup_inputs(seed: int = 0) -> dict:
    keys = jax.random.split(jax.random.key(seed), 2)
    turbulence = noise(keys[0], (NZ, NX, NY), 1.0, 6.0, ((0, 8), (1, 8), (2, 8)), jnp.float32)
    return {"turbulence": turbulence}


lift_alpha = -1.586134342059924
lift_beta = -0.052980118572961
lift_gamma = 0.882911075530934
lift_delta = 0.443506852043971
lift_zeta = 1.149604398860241
inverse_zeta = 1.0 / 1.149604398860241


def join_pairs(even_part, odd_part, direction):
    merged = jnp.stack([even_part, odd_part], axis=direction + 1)
    new_shape = list(even_part.shape)
    new_shape[direction] = new_shape[direction] * 2
    return merged.reshape(new_shape)


def lift_along(values, direction):
    length = values.shape[direction]
    even_part = lax.slice_in_dim(values, 0, length, 2, direction)
    odd_part = lax.slice_in_dim(values, 1, length, 2, direction)

    def shifted_next(operand):
        return jnp.roll(operand, -1, axis=direction)

    def shifted_prev(operand):
        return jnp.roll(operand, 1, axis=direction)

    odd_part = odd_part + lift_alpha * (even_part + shifted_next(even_part))
    even_part = even_part + lift_beta * (shifted_prev(odd_part) + odd_part)
    odd_part = odd_part + lift_gamma * (even_part + shifted_next(even_part))
    even_part = even_part + lift_delta * (shifted_prev(odd_part) + odd_part)
    return join_pairs(even_part * lift_zeta, odd_part * inverse_zeta, direction)


def place_inner(finer, coarse):
    full_shape = finer.shape
    sixfold = finer.reshape(full_shape[0] // 2, 2, full_shape[1] // 2, 2, full_shape[2] // 2, 2)
    inserted = coarse.reshape(full_shape[0] // 2, 1, full_shape[1] // 2, 1, full_shape[2] // 2, 1)
    sixfold = lax.dynamic_update_slice(sixfold, inserted, (0, 0, 0, 0, 0, 0))
    return sixfold.reshape(full_shape)


def reference(turbulence):
    finished_levels = []
    current = turbulence
    for level_index in range(LEVELS):
        for direction in range(3):
            current = lift_along(current, direction)
        finished_levels.append(current)
        current = lax.slice(current, (0, 0, 0), current.shape, (2, 2, 2))
    result = finished_levels[-1]
    for finer in reversed(finished_levels[:-1]):
        result = place_inner(finer, result)
    return result
```

```python
import functools
import itertools

import jax
import jax.numpy as jnp
import ml_dtypes
import numpy as np
from jax import lax
from jax.experimental import pallas as pl
from jax.experimental.pallas import tpu as pltpu
from jax.sharding import PartitionSpec as P

ALPHA = -1.586134342059924
BETA = -0.052980118572961
GAMMA = 0.882911075530934
DELTA = 0.443506852043971
ZETA = 1.149604398860241
AXES = ("gz", "gx", "gy")
BF16 = ml_dtypes.bfloat16


def lifting_matrix(n):
    v = np.eye(n)
    s, d = v[0::2].copy(), v[1::2].copy()
    d = d + ALPHA * (s + np.roll(s, -1, 0))
    s = s + BETA * (np.roll(d, 1, 0) + d)
    d = d + GAMMA * (s + np.roll(s, -1, 0))
    s = s + DELTA * (np.roll(d, 1, 0) + d)
    out = np.zeros((n, n))
    out[0::2], out[1::2] = s * ZETA, d / ZETA
    return out


def blocks(n, total):
    m, k, out = np.eye(total), total, []
    p = total // n // 2
    for level in range(3):
        t = lifting_matrix(k) @ m
        rows = t[p * k * n // total : (p + 1) * k * n // total]
        out.append([rows[:, (p + o) * n : (p + o + 1) * n] for o in (-1, 0, 1)])
        m, k = t[0::2], k // 2
    return out


def split(m):
    hi = m.astype(np.float32).astype(BF16)
    lo = (m - hi.astype(np.float64)).astype(np.float32).astype(BF16)
    return hi, lo


def low_rank(m, rank):
    u, s, v = np.linalg.svd(m, full_matrices=False)
    return u[:, :rank] * s[:rank], v[:rank]


def tables(n, total):
    per_level = blocks(n, total)
    place = np.zeros((2 * n, n + n // 2 + n // 4))
    place[np.arange(n), np.arange(n)] = 1
    place[n + 2 * np.arange(n // 2), n + np.arange(n // 2)] = 1
    place[n + 4 * np.arange(n // 4) + 1, n + n // 2 + np.arange(n // 4)] = 1
    before, own, after = (place @ np.concatenate([lv[o] for lv in per_level]) for o in range(3))
    r_before, s_before = low_rank(before, 6)
    r_after, s_after = low_rank(after, 6)
    send = np.zeros((16, n))
    send[0:6], send[8:14] = s_before, s_after
    take = np.zeros((16, 2 * n))
    take[0:6], take[8:14] = r_before.T, r_after.T
    w_hi, w_lo = split(own.T)
    t_hi, t_lo = split(take)
    ext = [np.concatenate([lv[1], lv[0][:8], lv[2][-8:]]) for lv in per_level]
    g1_hi, g1_lo = split(ext[0])
    g2_hi, g2_lo = split(np.concatenate(ext[1:]))
    return dict(
        wa=np.concatenate([w_hi, w_hi]),
        wb=w_lo,
        sa=np.concatenate(split(send)),
        ra=np.concatenate([t_hi, t_hi, t_lo]),
        g1a=np.concatenate([g1_hi, g1_hi], axis=1),
        g1b=g1_lo,
        g2a=np.concatenate([g2_hi, g2_hi], axis=1),
        g2b=g2_lo,
    )


def add(*terms):
    total = None
    for coefficient, v in terms:
        if v is None:
            continue
        v = v if coefficient == 1 else v * coefficient
        total = v if total is None else total + v
    return total


def plus(base, coefficient, one, two):
    pair = one if two is None else two if one is None else one + two
    return add((1, base), (coefficient, pair))


def lift_zero_extended(v, lowest, highest, low_only=False):
    a, b = lowest // 2 - 2, highest // 2 + 3
    s = {i: v.get(2 * i) for i in range(a, b + 1)}
    d = {i: v.get(2 * i + 1) for i in range(a, b + 1)}
    d1 = {i: plus(d[i], ALPHA, s[i], s[i + 1]) for i in range(a, b)}
    s1 = {i: plus(s[i], BETA, d1[i - 1], d1[i]) for i in range(a + 1, b)}
    d2 = {i: plus(d1[i], GAMMA, s1[i], s1[i + 1]) for i in range(a + 1, b - 1)}
    s2 = {i: plus(s1[i], DELTA, d2[i - 1], d2[i]) for i in range(a + 2, b - 1)}
    out = {}
    for i in range(a + 2, b - 1):
        for k, part, scale in ((2 * i, s2[i], ZETA), (2 * i + 1, d2[i], 1 / ZETA)):
            if lowest <= k <= highest and part is not None and not (low_only and k % 2):
                out[k] = part * scale
    return out, d1, s1


def halo_parts(v):
    bf = jnp.bfloat16
    hi = v.astype(bf)
    return hi, (v - hi.astype(jnp.float32)).astype(bf)


def dot(a, b, dims=((1,), (0,))):
    return lax.dot_general(a, b, (dims, ((), ())), preferred_element_type=jnp.float32)


def neighbour(offsets):
    return {
        axis: lax.rem(lax.axis_index(axis) + (o + lax.axis_size(axis)), lax.axis_size(axis))
        for axis, o in zip(AXES, offsets)
        if o
    }


SIDES = (1, -1)
TARGETS = (
    [(0, 0, c) for c in SIDES]
    + [(0, b, 0) for b in SIDES]
    + [(a, b, 0) for a in SIDES for b in (0, 1, -1)]
    + [(2 * a, b, 0) for a in SIDES for b in (0, 1, -1)]
)


def kernel(
    x, wa, wb, sa, ra, g1a, g1b, g2a, g2b, out,
    yc, q1, q2, q3, f2, f3,
    ys, yr, xs, xr, zs, zr, ps, pr, es, er, ds, dr, cs, cr,
    send_sem, recv_sem,
):
    barrier = pltpu.get_barrier_semaphore()
    for offsets in TARGETS:
        pl.semaphore_signal(barrier, inc=1, device_id=neighbour(offsets), device_id_type=pl.DeviceIdType.MESH)

    copies = []

    def send(source, target, offsets):
        k = len(copies)
        copy = pltpu.make_async_remote_copy(
            source, target, send_sem.at[k], recv_sem.at[k],
            device_id=neighbour(offsets), device_id_type=pl.DeviceIdType.MESH,
        )
        copies.append(copy)
        copy.start()
        return copy

    nz, nx, ny = x.shape

    v = x[...].reshape(nz * nx, ny)
    hi, lo = halo_parts(v)
    first = dot(sa[...], hi, ((1,), (1,)))
    second = dot(sa[0:16], lo, ((1,), (1,)))
    message = first[0:16] + first[16:32] + second
    ys[0] = message[0:8]
    ys[1] = message[8:16]
    pl.semaphore_wait(barrier, len(TARGETS))
    y_copies = [send(ys.at[k], yr.at[k], (0, 0, c)) for k, c in enumerate(SIDES)]

    for z in range(nz):
        hi, lo = halo_parts(x[z])
        yc[z] = dot(jnp.concatenate([hi, lo], axis=1), wa[...]) + dot(hi, wb[...])

    for copy in y_copies:
        copy.wait_recv()

    for z in range(nz):
        lanes = slice(z * nx, (z + 1) * nx)
        h_hi, h_lo = halo_parts(jnp.concatenate([yr[0, :, lanes], yr[1, :, lanes]], axis=0))
        y = yc[z] + dot(jnp.concatenate([h_hi, h_lo, h_hi], axis=0), ra[...], ((0,), (0,)))
        hi, lo = halo_parts(y)
        both = jnp.concatenate([hi, lo], axis=0)
        q1[z] = dot(g1a[...], both[:, 0:128]) + dot(g1b[...], hi[:, 0:128])
        q = dot(g2a[...], both[:, 128:256]) + dot(g2b[...], hi[:, 128:256])
        q2[z] = q[0:80]
        q3[z] = q[80:128]

    for tile in range(18):
        rows = slice(8 * tile, 8 * tile + 8)
        o, d1, s1 = lift_zero_extended({k: q1[k, rows] for k in range(nz)}, 0, nz - 1)
        s_first = q1[0, rows]
        to_next = (d1[nz // 2 - 1], s1[nz // 2 - 1])
        to_previous = (s_first, s_first + BETA * d1[0])
        for k in range(nz):
            if tile < 16:
                out[k, rows] = o[k]
            else:
                xs[tile - 16, k] = o[k]
        for a, pair in enumerate((to_next, to_previous)):
            for r in range(2):
                if tile < 16:
                    zs[a, r, rows] = pair[r]
                else:
                    es[2 * a + tile - 16, r] = pair[r]
    copies_late = [send(zs.at[a], zr.at[a], (s, 0, 0)) for a, s in enumerate(SIDES)]

    lane = lax.broadcasted_iota(jnp.int32, (8, 128), 1)

    def pack2(one, two):
        two = jnp.zeros_like(one) if two is None else pltpu.roll(two, 1, 1)
        return jnp.where(lane % 2 == 0, one, two)

    def pack4(parts):
        total = parts[0]
        for k, part in enumerate(parts[1:], 1):
            total = jnp.where(lane % 4 == (1 + k) % 4, pltpu.roll(part, k, 1), total)
        return total

    for tile in range(10):
        rows = slice(8 * tile, 8 * tile + 8)
        c2, _, _ = lift_zero_extended({k: q2[k, rows] for k in range(nz)}, -4, nz + 3, True)
        c2 = {k // 2: w for k, w in c2.items()}
        o, _, _ = lift_zero_extended(c2, -6, 12)
        for k in range(8):
            if tile < 8:
                f2[k, rows] = o[k]
            else:
                xs[tile - 8, 16 + k] = o[k]
        for a, pairs in enumerate((((8, 9), (10, 11), (12, None)), ((-6, -5), (-4, -3), (-2, -1)))):
            for r, (one, two) in enumerate(pairs):
                packed = pack2(o[one], None if two is None else o[two])
                if tile < 8:
                    ps[a, 64 * r + 8 * tile : 64 * r + 8 * tile + 8] = packed
                else:
                    es[2 * a + tile - 8, 2 + r] = packed

    for tile in range(6):
        rows = slice(8 * tile, 8 * tile + 8)
        c2, _, _ = lift_zero_extended({k: q3[k, rows] for k in range(nz)}, -4, nz + 3, True)
        c2 = {k // 2: w for k, w in c2.items()}
        c3, _, _ = lift_zero_extended(c2, -6, 12, True)
        c3 = {k // 2: w for k, w in c3.items()}
        o, _, _ = lift_zero_extended(c3, -6, 10)
        zero = jnp.zeros((8, 128), jnp.float32)
        for k in range(4):
            if tile < 4:
                f3[k, rows] = o[k]
            else:
                xs[tile - 4, 24 + k] = o[k]
        near = (pack4([o[4], o[5], o[6], o[7]]), pack4([o[-4], o[-3], o[-2], o[-1]]))
        far = (pack4([o[8], o[9], o[10], zero]), pack4([zero, zero, o[-6], o[-5]]))
        for a in range(2):
            if tile < 4:
                ps[a, 192 + 8 * tile : 200 + 8 * tile] = near[a]
                ds[a, rows] = far[a]
            else:
                es[2 * a + tile - 4, 5] = near[a]
                cs[2 * a + tile - 4] = far[a]

    for b, t in enumerate(SIDES):
        copies_late.append(send(xs.at[b], xr.at[b], (0, t, 0)))
    for a, s in enumerate(SIDES):
        copies_late.append(send(ps.at[a], pr.at[a], (s, 0, 0)))
        copies_late.append(send(ds.at[a], dr.at[a], (2 * s, 0, 0)))
        for b, t in enumerate(SIDES):
            copies_late.append(send(es.at[2 * a + b], er.at[2 * a + b], (s, t, 0)))
            copies_late.append(send(cs.at[2 * a + b], cr.at[2 * a + b], (2 * s, t, 0)))
    for copy in copies_late:
        copy.wait_recv()

    for a in range(2):
        for b, (r1, r2, r3) in enumerate(((0, 0, 0), (nx - 8, nx // 2 - 8, nx // 4 - 8))):
            e = 2 * a + b
            for r in range(2):
                zr[a, r, r1 : r1 + 8] += er[e, r]
            for r in range(3):
                pr[a, 64 * r + r2 : 64 * r + r2 + 8] += er[e, 2 + r]
            pr[a, 192 + r3 : 200 + r3] += er[e, 5]
            dr[a, r3 : r3 + 8] += cr[e]

    for b, (r1, r2, r3) in enumerate(((0, 0, 0), (nx - 8, nx // 2 - 8, nx // 4 - 8))):
        for k in range(16):
            out[k, r1 : r1 + 8] += xr[b, k]
        for k in range(8):
            f2[k, r2 : r2 + 8] += xr[b, 16 + k]
        for k in range(4):
            f3[k, r3 : r3 + 8] += xr[b, 24 + k]

    for tile in range(16):
        rows = slice(8 * tile, 8 * tile + 8)
        one, two = zr[0, 0, rows], zr[0, 1, rows]
        s10 = BETA * one
        d2m = one + GAMMA * (two + s10)
        d20 = GAMMA * s10
        s20 = s10 + DELTA * (d2m + d20)
        out[0, rows] += ZETA * s20
        out[1, rows] += (1 / ZETA) * d20
        out[2, rows] += (ZETA * DELTA) * d20
        one, two = zr[1, 0, rows], zr[1, 1, rows]
        d17 = ALPHA * one
        s17 = BETA * d17
        d27 = d17 + GAMMA * (s17 + two + s17)
        d26 = GAMMA * s17
        s27 = s17 + DELTA * (d26 + d27)
        out[12, rows] += (ZETA * DELTA) * d26
        out[13, rows] += (1 / ZETA) * d26
        out[14, rows] += ZETA * s27
        out[15, rows] += (1 / ZETA) * d27

    lane3 = lax.broadcasted_iota(jnp.int32, (32, 128), 1)
    lane2 = lax.broadcasted_iota(jnp.int32, (64, 128), 1)
    for k in range(8):
        total = f2[k]
        r, second = divmod(k, 2)
        if k < 5:
            part = pr[0, 64 * r : 64 * r + 64]
            total = total + (pltpu.roll(part, 127, 1) if second else part)
        if k >= 2:
            r, second = divmod(k - 2, 2)
            part = pr[1, 64 * r : 64 * r + 64]
            total = total + (pltpu.roll(part, 127, 1) if second else part)
        f2[k] = total
        if k % 2 == 0:
            j = k // 2
            packed = pr[0, 192:224] + pr[1, 192:224] + dr[0] + dr[1]
            deep = pltpu.roll(f3[j] + pltpu.roll(packed, (128 - j) % 128, 1), 127, 1)
            even = pl.ds(0, 32, 2)
            f2[k, even, :] = jnp.where(lane3 % 4 == 0, deep, f2[k, even, :])
        even = pl.ds(0, 64, 2)
        out[2 * k, even, :] = jnp.where(lane2 % 2 == 0, f2[k], out[2 * k, even, :])

    for copy in copies:
        copy.wait_send()


def local(turbulence, consts):
    nz, nx, ny = turbulence.shape
    f32 = jnp.float32
    vmem = lambda *shape: pltpu.VMEM(shape, f32)
    pair = lambda *shape: [vmem(*shape), vmem(*shape)]
    count = 18
    return pl.pallas_call(
        kernel,
        out_shape=jax.ShapeDtypeStruct(turbulence.shape, f32),
        in_specs=[pl.BlockSpec(memory_space=pltpu.VMEM)] * (1 + len(consts)),
        out_specs=pl.BlockSpec(memory_space=pltpu.VMEM),
        scratch_shapes=[
            vmem(nz, nx, 2 * ny), vmem(nz, 144, ny), vmem(nz, 80, ny), vmem(nz, 48, ny),
            vmem(8, 64, ny), vmem(4, 32, ny),
            *pair(2, 8, nz * nx),
            *pair(2, 28, 8, ny),
            *pair(2, 2, nx, ny),
            *pair(2, 224, ny),
            *pair(4, 6, 8, ny),
            *pair(2, 32, ny),
            *pair(4, 8, ny),
            pltpu.SemaphoreType.DMA((count,)),
            pltpu.SemaphoreType.DMA((count,)),
        ],
        compiler_params=pltpu.CompilerParams(collective_id=0, has_side_effects=True, vmem_limit_bytes=48 << 20),
    )(turbulence, *consts)


def solution(mesh):
    def run(turbulence):
        n = turbulence.shape[1]
        t = tables(n, n * lax.axis_size("gx"))
        return local(turbulence, [jnp.asarray(t[k]) for k in ("wa", "wb", "sa", "ra", "g1a", "g1b", "g2a", "g2b")])

    spec = P(*AXES)
    return jax.shard_map(run, mesh=mesh, in_specs=(spec,), out_specs=spec, check_vma=False)
```

```python
import functools
import itertools

import jax
import jax.numpy as jnp
import ml_dtypes
import numpy as np
from jax import lax
from jax.experimental import pallas as pl
from jax.experimental.pallas import tpu as pltpu
from jax.sharding import PartitionSpec as P

ALPHA = -1.586134342059924
BETA = -0.052980118572961
GAMMA = 0.882911075530934
DELTA = 0.443506852043971
ZETA = 1.149604398860241
AXES = ("gz", "gx", "gy")
BF16 = ml_dtypes.bfloat16


def lifting_matrix(n):
    v = np.eye(n)
    s, d = v[0::2].copy(), v[1::2].copy()
    d = d + ALPHA * (s + np.roll(s, -1, 0))
    s = s + BETA * (np.roll(d, 1, 0) + d)
    d = d + GAMMA * (s + np.roll(s, -1, 0))
    s = s + DELTA * (np.roll(d, 1, 0) + d)
    out = np.zeros((n, n))
    out[0::2], out[1::2] = s * ZETA, d / ZETA
    return out


def blocks(n, total):
    m, k, out = np.eye(total), total, []
    p = total // n // 2
    for level in range(3):
        t = lifting_matrix(k) @ m
        rows = t[p * k * n // total : (p + 1) * k * n // total]
        out.append([rows[:, (p + o) * n : (p + o + 1) * n] for o in (-1, 0, 1)])
        m, k = t[0::2], k // 2
    return out


def split(m):
    hi = m.astype(np.float32).astype(BF16)
    lo = (m - hi.astype(np.float64)).astype(np.float32).astype(BF16)
    return hi, lo


def low_rank(m, rank):
    u, s, v = np.linalg.svd(m, full_matrices=False)
    return u[:, :rank] * s[:rank], v[:rank]


def tables(n, total):
    per_level = blocks(n, total)
    place = np.zeros((2 * n, n + n // 2 + n // 4))
    place[np.arange(n), np.arange(n)] = 1
    place[n + 2 * np.arange(n // 2), n + np.arange(n // 2)] = 1
    place[n + 4 * np.arange(n // 4) + 1, n + n // 2 + np.arange(n // 4)] = 1
    before, own, after = (place @ np.concatenate([lv[o] for lv in per_level]) for o in range(3))
    r_before, s_before = low_rank(before, 6)
    r_after, s_after = low_rank(after, 6)
    send = np.zeros((16, n))
    send[0:6], send[8:14] = s_before, s_after
    take = np.zeros((16, 2 * n))
    take[0:6], take[8:14] = r_before.T, r_after.T
    w_hi, w_lo = split(own.T)
    t_hi, t_lo = split(take)
    ext = [np.concatenate([lv[1], lv[0][:8], lv[2][-8:]]) for lv in per_level]
    g1_hi, g1_lo = split(ext[0])
    g2_hi, g2_lo = split(np.concatenate(ext[1:]))
    return dict(
        wa=np.concatenate([w_hi, w_hi]),
        wb=w_lo,
        sa=np.concatenate(split(send)),
        ra=np.concatenate([t_hi, t_hi, t_lo]),
        g1a=np.concatenate([g1_hi, g1_hi], axis=1),
        g1b=g1_lo,
        g2a=np.concatenate([g2_hi, g2_hi], axis=1),
        g2b=g2_lo,
    )


def add(*terms):
    total = None
    for coefficient, v in terms:
        if v is None:
            continue
        v = v if coefficient == 1 else v * coefficient
        total = v if total is None else total + v
    return total


def plus(base, coefficient, one, two):
    pair = one if two is None else two if one is None else one + two
    return add((1, base), (coefficient, pair))


def lift_zero_extended(v, lowest, highest, low_only=False):
    a, b = lowest // 2 - 2, highest // 2 + 3
    s = {i: v.get(2 * i) for i in range(a, b + 1)}
    d = {i: v.get(2 * i + 1) for i in range(a, b + 1)}
    d1 = {i: plus(d[i], ALPHA, s[i], s[i + 1]) for i in range(a, b)}
    s1 = {i: plus(s[i], BETA, d1[i - 1], d1[i]) for i in range(a + 1, b)}
    d2 = {i: plus(d1[i], GAMMA, s1[i], s1[i + 1]) for i in range(a + 1, b - 1)}
    s2 = {i: plus(s1[i], DELTA, d2[i - 1], d2[i]) for i in range(a + 2, b - 1)}
    out = {}
    for i in range(a + 2, b - 1):
        for k, part, scale in ((2 * i, s2[i], ZETA), (2 * i + 1, d2[i], 1 / ZETA)):
            if lowest <= k <= highest and part is not None and not (low_only and k % 2):
                out[k] = part * scale
    return out, d1, s1


def halo_parts(v):
    bf = jnp.bfloat16
    hi = v.astype(bf)
    return hi, (v - hi.astype(jnp.float32)).astype(bf)


def dot(a, b, dims=((1,), (0,))):
    return lax.dot_general(a, b, (dims, ((), ())), preferred_element_type=jnp.float32)


def neighbour(offsets):
    return {
        axis: lax.rem(lax.axis_index(axis) + (o + lax.axis_size(axis)), lax.axis_size(axis))
        for axis, o in zip(AXES, offsets)
        if o
    }


SIDES = (1, -1)
TARGETS = (
    [(0, 0, c) for c in SIDES]
    + [(0, b, 0) for b in SIDES]
    + [(a, b, 0) for a in SIDES for b in (0, 1, -1)]
    + [(2 * a, b, 0) for a in SIDES for b in (0, 1, -1)]
)


def kernel(
    x_hbm, *rest
):
    tables_hbm, (out, x, *rest) = rest[:8], rest[8:]
    tables_vmem, rest = rest[:8], rest[8:]
    body(x_hbm, tables_hbm, out, x, tables_vmem, *rest)


def body(
    x_hbm, tables_hbm, out, x, tables_vmem, local_sem,
    yc, q1, q2, q3, f2, f3,
    ys, yr, xs, xr, zs, zr, ps, pr, es, er, ds, dr, cs, cr,
    send_sem, recv_sem,
):
    loads = [pltpu.make_async_copy(x_hbm, x, local_sem.at[0])]
    loads += [pltpu.make_async_copy(a, b, local_sem.at[k]) for k, (a, b) in enumerate(zip(tables_hbm, tables_vmem), 1)]
    for load in loads:
        load.start()
    sa, wa, wb, ra, g1a, g1b, g2a, g2b = tables_vmem
    barrier = pltpu.get_barrier_semaphore()
    for offsets in TARGETS:
        pl.semaphore_signal(barrier, inc=1, device_id=neighbour(offsets), device_id_type=pl.DeviceIdType.MESH)

    copies = []

    def send(source, target, offsets):
        k = len(copies)
        copy = pltpu.make_async_remote_copy(
            source, target, send_sem.at[k], recv_sem.at[k],
            device_id=neighbour(offsets), device_id_type=pl.DeviceIdType.MESH,
        )
        copies.append(copy)
        copy.start()
        return copy

    nz, nx, ny = x.shape

    with jax.named_scope("load"):
        for load in loads:
            load.wait()

    v = x[...].reshape(nz * nx, ny)
    hi, lo = halo_parts(v)
    first = dot(sa[...], hi, ((1,), (1,)))
    second = dot(sa[0:16], lo, ((1,), (1,)))
    message = first[0:16] + first[16:32] + second
    ys[0] = message[0:8]
    ys[1] = message[8:16]
    pl.semaphore_wait(barrier, len(TARGETS))
    y_copies = [send(ys.at[k], yr.at[k], (0, 0, c)) for k, c in enumerate(SIDES)]

    for z in range(nz):
        hi, lo = halo_parts(x[z])
        yc[z] = dot(jnp.concatenate([hi, lo], axis=1), wa[...]) + dot(hi, wb[...])

    for copy in y_copies:
        copy.wait_recv()

    for z in range(nz):
        lanes = slice(z * nx, (z + 1) * nx)
        h_hi, h_lo = halo_parts(jnp.concatenate([yr[0, :, lanes], yr[1, :, lanes]], axis=0))
        y = yc[z] + dot(jnp.concatenate([h_hi, h_lo, h_hi], axis=0), ra[...], ((0,), (0,)))
        hi, lo = halo_parts(y)
        both = jnp.concatenate([hi, lo], axis=0)
        q1[z] = dot(g1a[...], both[:, 0:128]) + dot(g1b[...], hi[:, 0:128])
        q = dot(g2a[...], both[:, 128:256]) + dot(g2b[...], hi[:, 128:256])
        q2[z] = q[0:80]
        q3[z] = q[80:128]

    for tile in range(18):
        rows = slice(8 * tile, 8 * tile + 8)
        o, d1, s1 = lift_zero_extended({k: q1[k, rows] for k in range(nz)}, 0, nz - 1)
        s_first = q1[0, rows]
        to_next = (d1[nz // 2 - 1], s1[nz // 2 - 1])
        to_previous = (s_first, s_first + BETA * d1[0])
        for k in range(nz):
            if tile < 16:
                out[k, rows] = o[k]
            else:
                xs[tile - 16, k] = o[k]
        for a, pair in enumerate((to_next, to_previous)):
            for r in range(2):
                if tile < 16:
                    zs[a, r, rows] = pair[r]
                else:
                    es[2 * a + tile - 16, r] = pair[r]
    copies_late = [send(zs.at[a], zr.at[a], (s, 0, 0)) for a, s in enumerate(SIDES)]

    lane = lax.broadcasted_iota(jnp.int32, (8, 128), 1)

    def pack2(one, two):
        two = jnp.zeros_like(one) if two is None else pltpu.roll(two, 1, 1)
        return jnp.where(lane % 2 == 0, one, two)

    def pack4(parts):
        total = parts[0]
        for k, part in enumerate(parts[1:], 1):
            total = jnp.where(lane % 4 == (1 + k) % 4, pltpu.roll(part, k, 1), total)
        return total

    for tile in range(10):
        rows = slice(8 * tile, 8 * tile + 8)
        c2, _, _ = lift_zero_extended({k: q2[k, rows] for k in range(nz)}, -4, nz + 3, True)
        c2 = {k // 2: w for k, w in c2.items()}
        o, _, _ = lift_zero_extended(c2, -6, 12)
        for k in range(8):
            if tile < 8:
                f2[k, rows] = o[k]
            else:
                xs[tile - 8, 16 + k] = o[k]
        for a, pairs in enumerate((((8, 9), (10, 11), (12, None)), ((-6, -5), (-4, -3), (-2, -1)))):
            for r, (one, two) in enumerate(pairs):
                packed = pack2(o[one], None if two is None else o[two])
                if tile < 8:
                    ps[a, 64 * r + 8 * tile : 64 * r + 8 * tile + 8] = packed
                else:
                    es[2 * a + tile - 8, 2 + r] = packed

    for tile in range(6):
        rows = slice(8 * tile, 8 * tile + 8)
        c2, _, _ = lift_zero_extended({k: q3[k, rows] for k in range(nz)}, -4, nz + 3, True)
        c2 = {k // 2: w for k, w in c2.items()}
        c3, _, _ = lift_zero_extended(c2, -6, 12, True)
        c3 = {k // 2: w for k, w in c3.items()}
        o, _, _ = lift_zero_extended(c3, -6, 10)
        zero = jnp.zeros((8, 128), jnp.float32)
        for k in range(4):
            if tile < 4:
                f3[k, rows] = o[k]
            else:
                xs[tile - 4, 24 + k] = o[k]
        near = (pack4([o[4], o[5], o[6], o[7]]), pack4([o[-4], o[-3], o[-2], o[-1]]))
        far = (pack4([o[8], o[9], o[10], zero]), pack4([zero, zero, o[-6], o[-5]]))
        for a in range(2):
            if tile < 4:
                ps[a, 192 + 8 * tile : 200 + 8 * tile] = near[a]
                ds[a, rows] = far[a]
            else:
                es[2 * a + tile - 4, 5] = near[a]
                cs[2 * a + tile - 4] = far[a]

    for b, t in enumerate(SIDES):
        copies_late.append(send(xs.at[b], xr.at[b], (0, t, 0)))
    for a, s in enumerate(SIDES):
        copies_late.append(send(ps.at[a], pr.at[a], (s, 0, 0)))
        copies_late.append(send(ds.at[a], dr.at[a], (2 * s, 0, 0)))
        for b, t in enumerate(SIDES):
            copies_late.append(send(es.at[2 * a + b], er.at[2 * a + b], (s, t, 0)))
            copies_late.append(send(cs.at[2 * a + b], cr.at[2 * a + b], (2 * s, t, 0)))
    for copy in copies_late:
        copy.wait_recv()

    for a in range(2):
        for b, (r1, r2, r3) in enumerate(((0, 0, 0), (nx - 8, nx // 2 - 8, nx // 4 - 8))):
            e = 2 * a + b
            for r in range(2):
                zr[a, r, r1 : r1 + 8] += er[e, r]
            for r in range(3):
                pr[a, 64 * r + r2 : 64 * r + r2 + 8] += er[e, 2 + r]
            pr[a, 192 + r3 : 200 + r3] += er[e, 5]
            dr[a, r3 : r3 + 8] += cr[e]

    for b, (r1, r2, r3) in enumerate(((0, 0, 0), (nx - 8, nx // 2 - 8, nx // 4 - 8))):
        for k in range(16):
            out[k, r1 : r1 + 8] += xr[b, k]
        for k in range(8):
            f2[k, r2 : r2 + 8] += xr[b, 16 + k]
        for k in range(4):
            f3[k, r3 : r3 + 8] += xr[b, 24 + k]

    for tile in range(16):
        rows = slice(8 * tile, 8 * tile + 8)
        one, two = zr[0, 0, rows], zr[0, 1, rows]
        s10 = BETA * one
        d2m = one + GAMMA * (two + s10)
        d20 = GAMMA * s10
        s20 = s10 + DELTA * (d2m + d20)
        out[0, rows] += ZETA * s20
        out[1, rows] += (1 / ZETA) * d20
        out[2, rows] += (ZETA * DELTA) * d20
        one, two = zr[1, 0, rows], zr[1, 1, rows]
        d17 = ALPHA * one
        s17 = BETA * d17
        d27 = d17 + GAMMA * (s17 + two + s17)
        d26 = GAMMA * s17
        s27 = s17 + DELTA * (d26 + d27)
        out[12, rows] += (ZETA * DELTA) * d26
        out[13, rows] += (1 / ZETA) * d26
        out[14, rows] += ZETA * s27
        out[15, rows] += (1 / ZETA) * d27

    lane3 = lax.broadcasted_iota(jnp.int32, (32, 128), 1)
    lane2 = lax.broadcasted_iota(jnp.int32, (64, 128), 1)
    for k in range(8):
        total = f2[k]
        r, second = divmod(k, 2)
        if k < 5:
            part = pr[0, 64 * r : 64 * r + 64]
            total = total + (pltpu.roll(part, 127, 1) if second else part)
        if k >= 2:
            r, second = divmod(k - 2, 2)
            part = pr[1, 64 * r : 64 * r + 64]
            total = total + (pltpu.roll(part, 127, 1) if second else part)
        f2[k] = total
        if k % 2 == 0:
            j = k // 2
            packed = pr[0, 192:224] + pr[1, 192:224] + dr[0] + dr[1]
            deep = pltpu.roll(f3[j] + pltpu.roll(packed, (128 - j) % 128, 1), 127, 1)
            even = pl.ds(0, 32, 2)
            f2[k, even, :] = jnp.where(lane3 % 4 == 0, deep, f2[k, even, :])
        even = pl.ds(0, 64, 2)
        out[2 * k, even, :] = jnp.where(lane2 % 2 == 0, f2[k], out[2 * k, even, :])

    for copy in copies:
        copy.wait_send()


def local(turbulence, consts):
    nz, nx, ny = turbulence.shape
    f32 = jnp.float32
    vmem = lambda *shape: pltpu.VMEM(shape, f32)
    pair = lambda *shape: [vmem(*shape), vmem(*shape)]
    count = 18
    return pl.pallas_call(
        kernel,
        out_shape=jax.ShapeDtypeStruct(turbulence.shape, f32),
        in_specs=[pl.BlockSpec(memory_space=pltpu.HBM)] * (1 + len(consts)),
        out_specs=pl.BlockSpec(memory_space=pltpu.VMEM),
        scratch_shapes=[
            vmem(nz, nx, ny),
            *[pltpu.VMEM(c.shape, c.dtype) for c in consts],
            pltpu.SemaphoreType.DMA((1 + len(consts),)),
            vmem(nz, nx, 2 * ny), vmem(nz, 144, ny), vmem(nz, 80, ny), vmem(nz, 48, ny),
            vmem(8, 64, ny), vmem(4, 32, ny),
            *pair(2, 8, nz * nx),
            *pair(2, 28, 8, ny),
            *pair(2, 2, nx, ny),
            *pair(2, 224, ny),
            *pair(4, 6, 8, ny),
            *pair(2, 32, ny),
            *pair(4, 8, ny),
            pltpu.SemaphoreType.DMA((count,)),
            pltpu.SemaphoreType.DMA((count,)),
        ],
        compiler_params=pltpu.CompilerParams(collective_id=0, has_side_effects=True, vmem_limit_bytes=48 << 20),
    )(*[pltpu.with_memory_space_constraint(a, pltpu.HBM) for a in (turbulence, *consts)])


def solution(mesh):
    def run(turbulence):
        n = turbulence.shape[1]
        t = tables(n, n * lax.axis_size("gx"))
        return local(turbulence, [jnp.asarray(t[k]) for k in ("sa", "wa", "wb", "ra", "g1a", "g1b", "g2a", "g2b")])

    spec = P(*AXES)
    return jax.shard_map(run, mesh=mesh, in_specs=(spec,), out_specs=spec, check_vma=False)
```

```python
import functools

import jax
import jax.numpy as jnp
import ml_dtypes
import numpy as np
from jax import lax
from jax.experimental import pallas as pl
from jax.experimental.pallas import tpu as pltpu
from jax.sharding import PartitionSpec as P

ALPHA = -1.586134342059924
BETA = -0.052980118572961
GAMMA = 0.882911075530934
DELTA = 0.443506852043971
ZETA = 1.149604398860241
AXES = ("gz", "gx", "gy")
BF16 = ml_dtypes.bfloat16


def lifting_matrix(n):
    v = np.eye(n)
    s, d = v[0::2].copy(), v[1::2].copy()
    d = d + ALPHA * (s + np.roll(s, -1, 0))
    s = s + BETA * (np.roll(d, 1, 0) + d)
    d = d + GAMMA * (s + np.roll(s, -1, 0))
    s = s + DELTA * (np.roll(d, 1, 0) + d)
    out = np.zeros((n, n))
    out[0::2], out[1::2] = s * ZETA, d / ZETA
    return out


def blocks(n, total):
    m, k, out = np.eye(total), total, []
    p = total // n // 2
    for level in range(3):
        t = lifting_matrix(k) @ m
        rows = t[p * k * n // total : (p + 1) * k * n // total]
        out.append([rows[:, (p + o) * n : (p + o + 1) * n] for o in (-1, 0, 1)])
        m, k = t[0::2], k // 2
    return out


def split(m):
    hi = m.astype(np.float32).astype(BF16)
    lo = (m - hi.astype(np.float64)).astype(np.float32).astype(BF16)
    return hi, lo


def low_rank(m, rank):
    u, s, v = np.linalg.svd(m, full_matrices=False)
    return u[:, :rank] * s[:rank], v[:rank]


def tables(n, total):
    per_level = blocks(n, total)
    place = np.zeros((2 * n, n + n // 2 + n // 4))
    place[np.arange(n), np.arange(n)] = 1
    place[n + 2 * np.arange(n // 2), n + np.arange(n // 2)] = 1
    place[n + 4 * np.arange(n // 4) + 1, n + n // 2 + np.arange(n // 4)] = 1
    before, own, after = (place @ np.concatenate([lv[o] for lv in per_level]) for o in range(3))
    r_before, s_before = low_rank(before, 6)
    r_after, s_after = low_rank(after, 6)
    send = np.zeros((16, n))
    send[0:6], send[8:14] = s_before, s_after
    take = np.zeros((16, 2 * n))
    take[0:6], take[8:14] = r_before.T, r_after.T
    w_hi, w_lo = split(own.T)
    t_hi, t_lo = split(take)
    ext = [np.concatenate([lv[1], lv[0][:w], lv[2][-w:]]) for lv, w in zip(per_level, (4, 8, 8))]
    g1_hi, g1_lo = split(ext[0])
    g2_hi, g2_lo = split(np.concatenate(ext[1:]))
    return dict(
        sa=np.concatenate(split(send)),
        wa=np.concatenate([w_hi, w_hi]),
        wb=w_lo,
        g1a=np.concatenate([g1_hi, g1_hi], axis=1),
        g1b=g1_lo,
        g2a=np.concatenate([g2_hi, g2_hi], axis=1),
        g2b=g2_lo,
        ra=np.concatenate([t_hi, t_hi, t_lo]),
    )


def level2_shares(n, total):
    before, _, after = blocks(n, total)[1]
    return before @ np.linalg.pinv(before[0:3]), after @ np.linalg.pinv(after[5:8])


def add(*terms):
    total = None
    for coefficient, v in terms:
        if v is None:
            continue
        v = v if coefficient == 1 else v * coefficient
        total = v if total is None else total + v
    return total


def plus(base, coefficient, one, two):
    pair = one if two is None else two if one is None else one + two
    return add((1, base), (coefficient, pair))


def lift_zero_extended(v, lowest, highest, low_only=False):
    a, b = lowest // 2 - 2, highest // 2 + 3
    s = {i: v.get(2 * i) for i in range(a, b + 1)}
    d = {i: v.get(2 * i + 1) for i in range(a, b + 1)}
    d1 = {i: plus(d[i], ALPHA, s[i], s[i + 1]) for i in range(a, b)}
    s1 = {i: plus(s[i], BETA, d1[i - 1], d1[i]) for i in range(a + 1, b)}
    d2 = {i: plus(d1[i], GAMMA, s1[i], s1[i + 1]) for i in range(a + 1, b - 1)}
    s2 = {i: plus(s1[i], DELTA, d2[i - 1], d2[i]) for i in range(a + 2, b - 1)}
    out = {}
    for i in range(a + 2, b - 1):
        for k, part, scale in ((2 * i, s2[i], ZETA), (2 * i + 1, d2[i], 1 / ZETA)):
            if lowest <= k <= highest and part is not None and not (low_only and k % 2):
                out[k] = part * scale
    return out, d1, s1


def halo_parts(v):
    bf = jnp.bfloat16
    hi = v.astype(bf)
    return hi, (v - hi.astype(jnp.float32)).astype(bf)


def dot(a, b, dims=((1,), (0,))):
    return lax.dot_general(a, b, (dims, ((), ())), preferred_element_type=jnp.float32)


def neighbour(offsets):
    return {
        axis: lax.rem(lax.axis_index(axis) + (o + lax.axis_size(axis)), lax.axis_size(axis))
        for axis, o in zip(AXES, offsets)
        if o
    }


SIDES = (1, -1)
TARGETS = (
    [(0, 0, c) for c in SIDES]
    + [(0, b, 0) for b in SIDES]
    + [(a, b, 0) for a in SIDES for b in (0, 1, -1)]
    + [(2 * a, b, 0) for a in SIDES for b in (0, 1, -1)]
)


def kernel(shares, x_hbm, *refs):
    tables_hbm, out, x, tables_vmem, rest = refs[:8], refs[8], refs[9], refs[10:18], refs[18:]
    (
        yc, q1, q2, q3, f2, f3, xc, ec,
        ys, yr, xs, xr, zs, zr, ts, tr, ps, pr, es, er, ds, dr, cs, cr,
        load_sem, send_sem, recv_sem,
    ) = rest
    nz, nx, ny = x.shape
    f32 = jnp.float32

    loads = [pltpu.make_async_copy(x_hbm, x, load_sem.at[0])]
    loads += [pltpu.make_async_copy(a, b, load_sem.at[k]) for k, (a, b) in enumerate(zip(tables_hbm, tables_vmem), 1)]
    for load in loads:
        load.start()
    sa, wa, wb, g1a, g1b, g2a, g2b, ra = tables_vmem
    barrier = pltpu.get_barrier_semaphore()
    for offsets in TARGETS:
        pl.semaphore_signal(barrier, inc=1, device_id=neighbour(offsets), device_id_type=pl.DeviceIdType.MESH)

    copies = []

    def send(source, target, offsets):
        k = len(copies)
        copy = pltpu.make_async_remote_copy(
            source, target, send_sem.at[k], recv_sem.at[k],
            device_id=neighbour(offsets), device_id_type=pl.DeviceIdType.MESH,
        )
        copies.append(copy)
        copy.start()
        return copy

    row = lax.broadcasted_iota(jnp.int32, (8, 128), 0)
    lane = lax.broadcasted_iota(jnp.int32, (8, 128), 1)

    def pack_rows(one, two, side):
        if side == 0:
            return jnp.where(row < 4, one, pltpu.roll(two, 4, 0))
        return jnp.where(row < 4, pltpu.roll(one, 4, 0), two)

    def unpack_rows(packed, second, side):
        v = packed if second == side else pltpu.roll(packed, 4, 0)
        return jnp.where((row < 4) == (side == 0), v, 0.0)

    def pack2(one, two):
        two = jnp.zeros_like(one) if two is None else pltpu.roll(two, 1, 1)
        return jnp.where(lane % 2 == 0, one, two)

    def pack4(parts):
        total = parts[0]
        for k, part in enumerate(parts[1:], 1):
            total = jnp.where(lane % 4 == (1 + k) % 4, pltpu.roll(part, k, 1), total)
        return total

    def shift(v, k):
        return pltpu.roll(v, 128 - k, 1) if k else v

    def lift_level1(v):
        o, d1, s1 = lift_zero_extended(v, 0, nz - 1)
        return o, ((d1[nz // 2 - 1], s1[nz // 2 - 1]), (v[0], v[0] + BETA * d1[0]))

    def expand(h, lanes):
        hi, lo = halo_parts(h)
        return dot(jnp.concatenate([hi, lo, hi], axis=0), ra[:, lanes], ((0,), (0,)))

    level1, deeper = slice(0, 128), slice(128, 256)

    with jax.named_scope("load"):
        loads[0].wait()
        loads[1].wait()

    with jax.named_scope("ymsg"):
        hi, lo = halo_parts(x[...].reshape(nz * nx, ny))
        first = dot(sa[...], hi, ((1,), (1,)))
        second = dot(sa[0:16], lo, ((1,), (1,)))
        message = first[0:16] + first[16:32] + second
        for z in range(nz):
            for c in range(2):
                ys[c, z] = message[8 * c : 8 * c + 8, z * nx : (z + 1) * nx]
    with jax.named_scope("barw"):
        pl.semaphore_wait(barrier, len(TARGETS))
        y_copies = [send(ys.at[k], yr.at[k], (0, 0, c)) for k, c in enumerate(SIDES)]

    with jax.named_scope("ycent"):
        for load in loads[2:]:
            load.wait()
        for z in range(nz):
            hi, lo = halo_parts(x[z])
            yc[z] = dot(jnp.concatenate([hi, lo], axis=1), wa[...]) + dot(hi, wb[...])
    with jax.named_scope("x1"):
        for z in range(nz):
            hi, lo = halo_parts(yc[z, :, level1])
            q1[z] = dot(g1a[...], jnp.concatenate([hi, lo], axis=0)) + dot(g1b[...], hi)
    with jax.named_scope("z1"):
        for tile in range(17):
            rows = slice(8 * tile, 8 * tile + 8)
            o, pairs = lift_level1({k: q1[k, rows] for k in range(nz)})
            for k in range(nz):
                if tile < 16:
                    out[k, rows] = o[k]
                else:
                    xc[k] = o[k]
            for a in range(2):
                for r in range(2):
                    if tile < 16:
                        zs[a, r, rows] = pairs[a][r]
                    else:
                        ec[a, r] = pairs[a][r]
        late = [send(zs.at[a], zr.at[a], (s, 0, 0)) for a, s in enumerate(SIDES)]
    with jax.named_scope("x2"):
        for z in range(nz):
            hi, lo = halo_parts(yc[z, :, deeper])
            q = dot(g2a[...], jnp.concatenate([hi, lo], axis=0)) + dot(g2b[...], hi)
            q2[z] = q[0:80]
            q3[z] = q[80:128]

    with jax.named_scope("ywait"):
        for copy in y_copies:
            copy.wait_recv()

    with jax.named_scope("halo"):
        h = jnp.concatenate([yr[0], yr[1]], axis=1).reshape(nz * 16, nx)
        hi, lo = halo_parts(h)
        both = jnp.concatenate([hi, lo], axis=1)
        rhs = ((1,), (1,))
        t1 = (dot(both, g1a[...], rhs) + dot(hi, g1b[...], rhs)).reshape(nz, 16, 136)
        t2 = (dot(both, g2a[...], rhs) + dot(hi, g2b[...], rhs)).reshape(nz, 16, 128)
        t1, t1_pairs = lift_level1({k: t1[k] for k in range(nz)})
        for a in range(2):
            for r in range(2):
                ts[a, r] = t1_pairs[a][r][:, 0:nx]
        for a, s in enumerate(SIDES):
            late.append(send(ts.at[a], tr.at[a], (s, 0, 0)))
    with jax.named_scope("q23"):
        for z in range(nz):
            q = expand(t2[z], deeper)
            q2[z] += q[0:80]
            q3[z] += q[80:128]

    with jax.named_scope("z23"):
        for tile in (8, 9, 0, 1, 2, 3, 4, 5, 6, 7):
            rows = slice(8 * tile, 8 * tile + 8)
            c2, _, _ = lift_zero_extended({k: q2[k, rows] for k in range(nz)}, -4, nz + 3, True)
            o, _, _ = lift_zero_extended({k // 2: w for k, w in c2.items()}, -3, 10)
            if tile < 8:
                for k in range(8):
                    f2[k, rows] = o[k]
            else:
                for k in range(4):
                    xs[tile - 8, 8 + k] = pack2(o[2 * k], o[2 * k + 1])
            for a, (one, two, three) in enumerate(((8, 9, 10), (-3, -2, -1))):
                for r, packed in enumerate((pack2(o[one], o[two]), pack2(o[three], None))):
                    if tile < 8:
                        ps[a, 64 * r + 8 * tile : 64 * r + 8 * tile + 8] = packed
                    else:
                        es[2 * a + tile - 8, 1 + r] = packed
        zero = jnp.zeros((8, 128), f32)
        for tile in range(6):
            rows = slice(8 * tile, 8 * tile + 8)
            c2, _, _ = lift_zero_extended({k: q3[k, rows] for k in range(nz)}, -4, nz + 3, True)
            c3, _, _ = lift_zero_extended({k // 2: w for k, w in c2.items()}, -6, 12, True)
            o, _, _ = lift_zero_extended({k // 2: w for k, w in c3.items()}, -6, 10)
            if tile < 4:
                for k in range(4):
                    f3[k, rows] = o[k]
            else:
                xs[tile - 4, 12] = pack4([o[0], o[1], o[2], o[3]])
            near = (pack4([o[4], o[5], o[6], o[7]]), pack4([o[-4], o[-3], o[-2], o[-1]]))
            far = (pack4([o[8], o[9], o[10], zero]), pack4([zero, zero, o[-6], o[-5]]))
            for a in range(2):
                if tile < 4:
                    ps[a, 128 + 8 * tile : 136 + 8 * tile] = near[a]
                    ds[a, rows] = far[a]
                else:
                    es[2 * a + tile - 4, 3] = near[a]
                    cs[2 * a + tile - 4] = far[a]
        for a, s in enumerate(SIDES):
            late.append(send(ds.at[a], dr.at[a], (2 * s, 0, 0)))
            late.append(send(ps.at[a], pr.at[a], (s, 0, 0)))
            for b, t in enumerate(SIDES):
                late.append(send(cs.at[2 * a + b], cr.at[2 * a + b], (2 * s, t, 0)))

    with jax.named_scope("xs"):
        full = [xc[k] + expand(t1[k][:, nx : nx + 8], level1) for k in range(nz)]
        for k in range(nz // 2):
            for b in range(2):
                xs[b, k] = pack_rows(full[2 * k], full[2 * k + 1], b)
        for a in range(2):
            full = [ec[a, r] + expand(t1_pairs[a][r][:, nx : nx + 8], level1) for r in range(2)]
            for b in range(2):
                es[2 * a + b, 0] = pack_rows(full[0], full[1], b)
        for b, t in enumerate(SIDES):
            late.append(send(xs.at[b], xr.at[b], (0, t, 0)))
            for a, s in enumerate(SIDES):
                late.append(send(es.at[2 * a + b], er.at[2 * a + b], (s, t, 0)))

    with jax.named_scope("own1"):
        for k in range(nz):
            out[k] += expand(t1[k][:, 0:nx], level1)

    with jax.named_scope("wait2"):
        for copy in late:
            copy.wait_recv()

    with jax.named_scope("edges"):
        for a in range(2):
            for r in range(2):
                zr[a, r] += expand(tr[a, r], level1)
            for b, (r1, r2, r3) in enumerate(((0, 0, 0), (nx - 8, nx // 2 - 8, nx // 4 - 8))):
                e = 2 * a + b
                for r in range(2):
                    zr[a, r, r1 : r1 + 8] += unpack_rows(er[e, 0], r, b)
                    pr[a, 64 * r + r2 : 64 * r + r2 + 8] += er[e, 1 + r]
                pr[a, 128 + r3 : 136 + r3] += er[e, 3]
                dr[a, r3 : r3 + 8] += cr[e]

    with jax.named_scope("xfaces"):
        for b, (r1, r2, r3) in enumerate(((0, 0, 0), (nx - 8, nx // 2 - 8, nx // 4 - 8))):
            for k in range(16):
                out[k, r1 : r1 + 8] += unpack_rows(xr[b, k // 2], k % 2, b)
            for k in range(8):
                f2[k, r2 : r2 + 8] += shift(xr[b, 8 + k // 2], k % 2)
            for k in range(4):
                f3[k, r3 : r3 + 8] += shift(xr[b, 12], k)

    with jax.named_scope("zfaces"):
        for tile in range(16):
            rows = slice(8 * tile, 8 * tile + 8)
            one, two = zr[0, 0, rows], zr[0, 1, rows]
            s10 = BETA * one
            d2m = one + GAMMA * (two + s10)
            d20 = GAMMA * s10
            s20 = s10 + DELTA * (d2m + d20)
            out[0, rows] += ZETA * s20
            out[1, rows] += (1 / ZETA) * d20
            out[2, rows] += (ZETA * DELTA) * d20
            one, two = zr[1, 0, rows], zr[1, 1, rows]
            d17 = ALPHA * one
            s17 = BETA * d17
            d27 = d17 + GAMMA * (s17 + two + s17)
            d26 = GAMMA * s17
            s27 = s17 + DELTA * (d26 + d27)
            out[nz - 4, rows] += (ZETA * DELTA) * d26
            out[nz - 3, rows] += (1 / ZETA) * d26
            out[nz - 2, rows] += ZETA * s27
            out[nz - 1, rows] += (1 / ZETA) * d27

    with jax.named_scope("final"):
        lane3 = lax.broadcasted_iota(jnp.int32, (32, 128), 1)
        lane2 = lax.broadcasted_iota(jnp.int32, (64, 128), 1)
        parts = []
        for a in range(2):
            first, second = pr[a, 0:64], pr[a, 64:128]
            parts.append((first, shift(first, 1), second))
        deep = pr[0, 128:160] + pr[1, 128:160] + dr[0] + dr[1]
        for k in range(8):
            total = f2[k]
            for a in range(2):
                total = add((1, total), *[(float(shares[a][k, r]), parts[a][r]) for r in range(3) if abs(shares[a][k, r]) > 1e-12])
            f2[k] = total
            if k % 2 == 0:
                j = k // 2
                even = pl.ds(0, 32, 2)
                f2[k, even, :] = jnp.where(lane3 % 4 == 0, shift(f3[j], 1) + shift(deep, 1 + j), f2[k, even, :])
            even = pl.ds(0, 64, 2)
            out[2 * k, even, :] = jnp.where(lane2 % 2 == 0, f2[k], out[2 * k, even, :])

    with jax.named_scope("sendwait"):
        for copy in copies:
            copy.wait_send()


def local(turbulence, consts, shares):
    nz, nx, ny = turbulence.shape
    f32 = jnp.float32
    vmem = lambda *shape: pltpu.VMEM(shape, f32)
    pair = lambda *shape: [vmem(*shape), vmem(*shape)]
    count = 20
    return pl.pallas_call(
        functools.partial(kernel, shares),
        out_shape=jax.ShapeDtypeStruct(turbulence.shape, f32),
        in_specs=[pl.BlockSpec(memory_space=pltpu.HBM)] * (1 + len(consts)),
        out_specs=pl.BlockSpec(memory_space=pltpu.VMEM),
        scratch_shapes=[
            vmem(nz, nx, ny),
            *[pltpu.VMEM(c.shape, c.dtype) for c in consts],
            vmem(nz, nx, 2 * ny), vmem(nz, 136, ny), vmem(nz, 80, ny), vmem(nz, 48, ny),
            vmem(8, 64, ny), vmem(4, 32, ny),
            vmem(nz, 8, ny), vmem(2, 2, 8, ny),
            *pair(2, nz, 8, nx),
            *pair(2, 13, 8, ny),
            *pair(2, 2, nx, ny),
            *pair(2, 2, 16, nx),
            *pair(2, 160, ny),
            *pair(4, 4, 8, ny),
            *pair(2, 32, ny),
            *pair(4, 8, ny),
            pltpu.SemaphoreType.DMA((1 + len(consts),)),
            pltpu.SemaphoreType.DMA((count,)),
            pltpu.SemaphoreType.DMA((count,)),
        ],
        compiler_params=pltpu.CompilerParams(collective_id=0, has_side_effects=True, vmem_limit_bytes=48 << 20),
    )(*[pltpu.with_memory_space_constraint(a, pltpu.HBM) for a in (turbulence, *consts)])


def solution(mesh):
    def run(turbulence):
        nz, n, _ = turbulence.shape
        t = tables(n, n * lax.axis_size("gx"))
        names = ("sa", "wa", "wb", "g1a", "g1b", "g2a", "g2b", "ra")
        return local(turbulence, [jnp.asarray(t[k]) for k in names], level2_shares(nz, nz * lax.axis_size("gz")))

    spec = P(*AXES)
    return jax.shard_map(run, mesh=mesh, in_specs=(spec,), out_specs=spec, check_vma=False)
```

```python
import functools

import jax
import jax.numpy as jnp
import ml_dtypes
import numpy as np
from jax import lax
from jax.experimental import pallas as pl
from jax.experimental.pallas import tpu as pltpu
from jax.sharding import PartitionSpec as P

ALPHA = -1.586134342059924
BETA = -0.052980118572961
GAMMA = 0.882911075530934
DELTA = 0.443506852043971
ZETA = 1.149604398860241
AXES = ("gz", "gx", "gy")
BF16 = ml_dtypes.bfloat16


def lifting_matrix(n):
    v = np.eye(n)
    s, d = v[0::2].copy(), v[1::2].copy()
    d = d + ALPHA * (s + np.roll(s, -1, 0))
    s = s + BETA * (np.roll(d, 1, 0) + d)
    d = d + GAMMA * (s + np.roll(s, -1, 0))
    s = s + DELTA * (np.roll(d, 1, 0) + d)
    out = np.zeros((n, n))
    out[0::2], out[1::2] = s * ZETA, d / ZETA
    return out


def blocks(n, total):
    m, k, out = np.eye(total), total, []
    p = total // n // 2
    for level in range(3):
        t = lifting_matrix(k) @ m
        rows = t[p * k * n // total : (p + 1) * k * n // total]
        out.append([rows[:, (p + o) * n : (p + o + 1) * n] for o in (-1, 0, 1)])
        m, k = t[0::2], k // 2
    return out


def split(m):
    hi = m.astype(np.float32).astype(BF16)
    lo = (m - hi.astype(np.float64)).astype(np.float32).astype(BF16)
    return hi, lo


def low_rank(m, first, rank, rank_first):
    v = np.linalg.svd(m[:first])[2][:rank_first]
    rest = np.linalg.svd(m - m @ v.T @ v)[2][: rank - rank_first]
    v = np.concatenate([v, rest])
    left = m @ v.T
    left[:first, rank_first:] = 0
    return left, v


def tables(n, total):
    per_level = blocks(n, total)
    place = np.zeros((2 * n, n + n // 2 + n // 4))
    place[np.arange(n), np.arange(n)] = 1
    place[n + 2 * np.arange(n // 2), n + np.arange(n // 2)] = 1
    place[n + 4 * np.arange(n // 4) + 1, n + n // 2 + np.arange(n // 4)] = 1
    before, own, after = (place @ np.concatenate([lv[o] for lv in per_level]) for o in range(3))
    r_before, s_before = low_rank(before, n, 6, 2)
    r_after, s_after = low_rank(after, n, 6, 2)
    send = np.zeros((16, n))
    send[0:6], send[8:14] = s_before, s_after
    take = np.zeros((16, 2 * n))
    take[0:6], take[8:14] = r_before.T, r_after.T
    w_hi, w_lo = split(own.T)
    t_hi, t_lo = split(take)
    ext = [np.concatenate([lv[1], lv[0][:w], lv[2][-w:]]) for lv, w in zip(per_level, (4, 8, 8))]
    g1_hi, g1_lo = split(ext[0])
    g2_hi, g2_lo = split(np.concatenate(ext[1:]))
    return dict(
        sa=np.concatenate(split(send)),
        wa=np.concatenate([w_hi, w_hi]),
        wb=w_lo,
        g1a=np.concatenate([g1_hi, g1_hi], axis=1),
        g1b=g1_lo,
        g2a=np.concatenate([g2_hi, g2_hi], axis=1),
        g2b=g2_lo,
        ra=np.concatenate([t_hi, t_hi, t_lo]),
    )


def level2_shares(n, total):
    before, _, after = blocks(n, total)[1]
    return before @ np.linalg.pinv(before[0:3]), after @ np.linalg.pinv(after[5:8])


def level3_shares(n, total):
    m = np.eye(total)
    for k in (total, total // 2, total // 4):
        rows = lifting_matrix(k) @ m
        m = rows[0::2]
    p = total // n // 2
    far = rows[p * n // 4 : (p + 1) * n // 4, (p - 2) * n : (p - 1) * n]
    return (far @ np.linalg.pinv(far[0:2]))[2]


def add(*terms):
    total = None
    for coefficient, v in terms:
        if v is None:
            continue
        v = v if coefficient == 1 else v * coefficient
        total = v if total is None else total + v
    return total


def plus(base, coefficient, one, two):
    pair = one if two is None else two if one is None else one + two
    return add((1, base), (coefficient, pair))


def lift_zero_extended(v, lowest, highest, low_only=False):
    a, b = lowest // 2 - 2, highest // 2 + 3
    s = {i: v.get(2 * i) for i in range(a, b + 1)}
    d = {i: v.get(2 * i + 1) for i in range(a, b + 1)}
    d1 = {i: plus(d[i], ALPHA, s[i], s[i + 1]) for i in range(a, b)}
    s1 = {i: plus(s[i], BETA, d1[i - 1], d1[i]) for i in range(a + 1, b)}
    d2 = {i: plus(d1[i], GAMMA, s1[i], s1[i + 1]) for i in range(a + 1, b - 1)}
    s2 = {i: plus(s1[i], DELTA, d2[i - 1], d2[i]) for i in range(a + 2, b - 1)}
    out = {}
    for i in range(a + 2, b - 1):
        for k, part, scale in ((2 * i, s2[i], ZETA), (2 * i + 1, d2[i], 1 / ZETA)):
            if lowest <= k <= highest and part is not None and not (low_only and k % 2):
                out[k] = part * scale
    return out, d1, s1


def halo_parts(v):
    bf = jnp.bfloat16
    hi = v.astype(bf)
    return hi, (v - hi.astype(jnp.float32)).astype(bf)


def dot(a, b, dims=((1,), (0,))):
    return lax.dot_general(a, b, (dims, ((), ())), preferred_element_type=jnp.float32)


def neighbour(offsets):
    return {
        axis: lax.rem(lax.axis_index(axis) + (o + lax.axis_size(axis)), lax.axis_size(axis))
        for axis, o in zip(AXES, offsets)
        if o
    }


SIDES = (1, -1)
TARGETS = (
    [(a, b, 0) for a in (2, -2, 1, -1, 0) for b in SIDES]
    + [(a, 0, 0) for a in (2, -2, 1, -1)]
    + [(0, 0, c) for c in SIDES]
)


def kernel(shares, far_share, x_hbm, *refs):
    tables_hbm, out, x, tables_vmem, rest = refs[:8], refs[8], refs[9], refs[10:18], refs[18:]
    (
        yc, q1, q2, q3, f2, f3, xc, ec,
        ys, yr, xs, xr, zs, zr, ts, tr, ps, pr, es, er, ds, dr, cs, cr,
        load_sem, send_sem, recv_sem,
    ) = rest
    nz, nx, ny = x.shape
    f32 = jnp.float32

    loads = [pltpu.make_async_copy(x_hbm, x, load_sem.at[0])]
    loads += [pltpu.make_async_copy(a, b, load_sem.at[k]) for k, (a, b) in enumerate(zip(tables_hbm, tables_vmem), 1)]
    for load in loads[:2]:
        load.start()
    sa, wa, wb, g1a, g1b, g2a, g2b, ra = tables_vmem
    barrier = pltpu.get_barrier_semaphore()
    for offsets in TARGETS:
        pl.semaphore_signal(barrier, inc=1, device_id=neighbour(offsets), device_id_type=pl.DeviceIdType.MESH)
    for load in loads[2:]:
        load.start()

    copies = []

    def send(source, target, offsets):
        k = len(copies)
        copy = pltpu.make_async_remote_copy(
            source, target, send_sem.at[k], recv_sem.at[k],
            device_id=neighbour(offsets), device_id_type=pl.DeviceIdType.MESH,
        )
        copies.append(copy)
        copy.start()
        return copy

    row = lax.broadcasted_iota(jnp.int32, (8, 128), 0)
    lane = lax.broadcasted_iota(jnp.int32, (8, 128), 1)

    def pack_rows(one, two, side):
        if side == 0:
            return jnp.where(row < 4, one, pltpu.roll(two, 4, 0))
        return jnp.where(row < 4, pltpu.roll(one, 4, 0), two)

    def unpack_rows(packed, second, side):
        v = packed if second == side else pltpu.roll(packed, 4, 0)
        return jnp.where((row < 4) == (side == 0), v, 0.0)

    def pack2(one, two):
        two = jnp.zeros_like(one) if two is None else pltpu.roll(two, 1, 1)
        return jnp.where(lane % 2 == 0, one, two)

    def pack4(parts):
        total = parts[0]
        for k, part in enumerate(parts[1:], 1):
            total = jnp.where(lane % 4 == (1 + k) % 4, pltpu.roll(part, k, 1), total)
        return total

    def shift(v, k):
        return pltpu.roll(v, 128 - k, 1) if k else v

    def lift_level1(v):
        o, d1, s1 = lift_zero_extended(v, 0, nz - 1)
        return o, ((d1[nz // 2 - 1], s1[nz // 2 - 1]), (v[0], v[0] + BETA * d1[0]))

    def expand(h, lanes):
        hi, lo = halo_parts(h)
        return dot(jnp.concatenate([hi, lo, hi], axis=0), ra[:, lanes], ((0,), (0,)))

    level1, deeper = slice(0, 128), slice(128, 256)

    with jax.named_scope("load"):
        loads[0].wait()
        loads[1].wait()

    with jax.named_scope("ymsg"):
        hi, lo = halo_parts(x[...].reshape(nz * nx, ny))
        first = dot(sa[...], hi, ((1,), (1,)))
        second = dot(sa[0:16], lo, ((1,), (1,)))
        message = first[0:16] + first[16:32] + second
        for z in range(nz):
            for c in range(2):
                ys[c, z] = message[8 * c : 8 * c + 8, z * nx : (z + 1) * nx]
    with jax.named_scope("barw"):
        for tile in range(16):
            rows = slice(8 * tile, 8 * tile + 8)
            v = {k: x[k, rows] for k in (0, 1, 2, nz - 4, nz - 3, nz - 2, nz - 1)}
            last = v[nz - 1] + ALPHA * v[nz - 2]
            zs[0, 0, rows] = last
            zs[0, 1, rows] = v[nz - 2] + BETA * (v[nz - 3] + ALPHA * (v[nz - 4] + v[nz - 2]) + last)
            zs[1, 0, rows] = v[0]
            zs[1, 1, rows] = v[0] + BETA * (v[1] + ALPHA * (v[0] + v[2]))
        pl.semaphore_wait(barrier, len(TARGETS))
        y_copies = [send(ys.at[k], yr.at[k], (0, 0, c)) for k, c in enumerate(SIDES)]
        z_copies = [send(zs.at[a], zr.at[a], (s, 0, 0)) for a, s in enumerate(SIDES)]

    with jax.named_scope("ycent"):
        for load in loads[2:]:
            load.wait()
        for z in range(nz):
            hi, lo = halo_parts(x[z])
            yc[z] = dot(jnp.concatenate([hi, lo], axis=1), wa[...]) + dot(hi, wb[...])
    with jax.named_scope("x1"):
        for z in range(nz):
            hi, lo = halo_parts(yc[z, :, level1])
            q1[z] = dot(g1a[...], jnp.concatenate([hi, lo], axis=0)) + dot(g1b[...], hi)
    with jax.named_scope("z1"):
        for tile in range(17):
            rows = slice(8 * tile, 8 * tile + 8)
            o, pairs = lift_level1({k: q1[k, rows] for k in range(nz)})
            for k in range(nz):
                if tile < 16:
                    out[k, rows] = o[k]
                else:
                    xc[k] = o[k]
            if tile == 16:
                for a in range(2):
                    for r in range(2):
                        ec[a, r] = pairs[a][r]
        late = []
    with jax.named_scope("x2"):
        for z in range(nz):
            hi, lo = halo_parts(yc[z, :, deeper])
            q = dot(g2a[...], jnp.concatenate([hi, lo], axis=0)) + dot(g2b[...], hi)
            q2[z] = q[0:80]
            q3[z] = q[80:128]

    with jax.named_scope("ywait"):
        for copy in y_copies:
            copy.wait_recv()

    with jax.named_scope("halo"):
        h = jnp.concatenate([yr[0], yr[1]], axis=1).reshape(nz * 16, nx)
        hi, lo = halo_parts(h)
        both = jnp.concatenate([hi, lo], axis=1)
        rhs = ((1,), (1,))
        t1 = (dot(both, g1a[...], rhs) + dot(hi, g1b[...], rhs)).reshape(nz, 16, 136)
        t2 = (dot(both, g2a[...], rhs) + dot(hi, g2b[...], rhs)).reshape(nz, 16, 128)
        t1, t1_pairs = lift_level1({k: t1[k] for k in range(nz)})
        for a in range(2):
            (one, two), (three, four) = ((t[0:8, 0:nx], t[8:16, 0:nx]) for t in t1_pairs[a])
            second, fourth = jnp.where(row < 2, one, pltpu.roll(two, 2, 0)), jnp.where(row < 2, three, pltpu.roll(four, 2, 0))
            ts[a] = jnp.where(row < 4, second, pltpu.roll(fourth, 4, 0))
        for a, s in enumerate(SIDES):
            late.append(send(ts.at[a], tr.at[a], (s, 0, 0)))
    with jax.named_scope("q23"):
        for z in range(nz):
            q = expand(t2[z], deeper)
            q2[z] += q[0:80]
            q3[z] += q[80:128]

    with jax.named_scope("z23"):
        for tile in (8, 9, 0, 1, 2, 3, 4, 5, 6, 7):
            rows = slice(8 * tile, 8 * tile + 8)
            c2, _, _ = lift_zero_extended({k: q2[k, rows] for k in range(nz)}, -4, nz + 3, True)
            o, _, _ = lift_zero_extended({k // 2: w for k, w in c2.items()}, -3, 10)
            if tile < 8:
                for k in range(8):
                    f2[k, rows] = o[k]
            else:
                for k in range(4):
                    xs[tile - 8, 8 + k] = pack2(o[2 * k], o[2 * k + 1])
            for a, (one, two, three) in enumerate(((8, 9, 10), (-3, -2, -1))):
                for r, packed in enumerate((pack2(o[one], o[two]), pack2(o[three], None))):
                    if tile < 8:
                        ps[a, 64 * r + 8 * tile : 64 * r + 8 * tile + 8] = packed
                    else:
                        es[2 * a + tile - 8, 1 + r] = packed
        kept = {}
        for tile in range(6):
            rows = slice(8 * tile, 8 * tile + 8)
            c2, _, _ = lift_zero_extended({k: q3[k, rows] for k in range(nz)}, -4, nz + 3, True)
            c3, _, _ = lift_zero_extended({k // 2: w for k, w in c2.items()}, -6, 12, True)
            o, _, _ = lift_zero_extended({k // 2: w for k, w in c3.items()}, -6, 10)
            if tile < 4:
                for k in range(4):
                    f3[k, rows] = o[k]
            else:
                xs[tile - 4, 12] = pack4([o[0], o[1], o[2], o[3]])
            near = ((o[4], o[5], o[6], o[7]), (o[-4], o[-3], o[-2], o[-1]))
            far = ((o[8], o[9]), (o[-6], o[-5]))
            for a in range(2):
                if tile < 4:
                    for half in range(2):
                        at = slice(64 + 32 * half + 8 * tile, 72 + 32 * half + 8 * tile)
                        one, two = near[a][2 * half], near[a][2 * half + 1]
                        odd = jnp.where(lane % 4 == 1, one, pltpu.roll(two, 2, 1))
                        ps[a, at] = jnp.where(lane % 2 == 0, ps[a, at], odd)
                    if tile < 2:
                        kept[a, tile] = far[a]
                    else:
                        ds[a, 8 * tile - 16 : 8 * tile - 8] = pack4([*kept[a, tile - 2], *far[a]])
                else:
                    es[2 * a + tile - 4, 3] = pack4(near[a])
                    cs[2 * a + tile - 4] = pack4([*far[a], *far[a]])
        for a, s in enumerate(SIDES):
            late.append(send(ds.at[a], dr.at[a], (2 * s, 0, 0)))
            late.append(send(ps.at[a], pr.at[a], (s, 0, 0)))
            for b, t in enumerate(SIDES):
                late.append(send(cs.at[2 * a + b], cr.at[2 * a + b], (2 * s, t, 0)))

    with jax.named_scope("xs"):
        full = [xc[k] + expand(t1[k][:, nx : nx + 8], level1) for k in range(nz)]
        for k in range(nz // 2):
            for b in range(2):
                xs[b, k] = pack_rows(full[2 * k], full[2 * k + 1], b)
        for a in range(2):
            full = [ec[a, r] + expand(t1_pairs[a][r][:, nx : nx + 8], level1) for r in range(2)]
            for b in range(2):
                es[2 * a + b, 0] = pack_rows(full[0], full[1], b)
        for b, t in enumerate(SIDES):
            late.append(send(xs.at[b], xr.at[b], (0, t, 0)))
            for a, s in enumerate(SIDES):
                late.append(send(es.at[2 * a + b], er.at[2 * a + b], (s, t, 0)))

    with jax.named_scope("own1"):
        for k in range(nz):
            out[k] += expand(t1[k][:, 0:nx], level1)

    with jax.named_scope("zraw"):
        for copy in z_copies:
            copy.wait_recv()
        for a in range(2):
            for r in range(2):
                hi, lo = halo_parts(zr[a, r])
                y = dot(jnp.concatenate([hi, lo], axis=1), wa[:, level1]) + dot(hi, wb[:, level1])
                hi, lo = halo_parts(y)
                zr[a, r] = dot(g1a[0:nx], jnp.concatenate([hi, lo], axis=0)) + dot(g1b[0:nx], hi)

    with jax.named_scope("wait2"):
        for copy in late:
            copy.wait_recv()

    def take_far(a, rows, v, first):
        one, two = shift(v, first), shift(v, first + 1)
        if a == 0:
            f3[0, rows] += one
            f3[1, rows] += two
            f3[2, rows] += float(far_share[0]) * one + float(far_share[1]) * two
        else:
            f3[2, rows] += one
            f3[3, rows] += two

    with jax.named_scope("edges"):
        for a in range(2):
            for r in range(2):
                quad = pltpu.roll(tr[a], 4, 0) if r else tr[a]
                quad = [jnp.where(row < 2, pltpu.roll(quad, 6, 0) if c else quad, 0.0) for c in range(2)]
                zr[a, r] += expand(jnp.concatenate(quad, axis=0), level1)
            for b, (r1, r2, r3) in enumerate(((0, 0, 0), (nx - 8, nx // 2 - 8, nx // 4 - 8))):
                e = 2 * a + b
                for r in range(2):
                    zr[a, r, r1 : r1 + 8] += unpack_rows(er[e, 0], r, b)
                    pr[a, 64 * r + r2 : 64 * r + r2 + 8] += er[e, 1 + r]
                for j in range(4):
                    f3[j, r3 : r3 + 8] += shift(er[e, 3], j)
                take_far(a, slice(r3, r3 + 8), cr[e], 0)

    with jax.named_scope("xfaces"):
        for b, (r1, r2, r3) in enumerate(((0, 0, 0), (nx - 8, nx // 2 - 8, nx // 4 - 8))):
            for k in range(16):
                out[k, r1 : r1 + 8] += unpack_rows(xr[b, k // 2], k % 2, b)
            for k in range(8):
                f2[k, r2 : r2 + 8] += shift(xr[b, 8 + k // 2], k % 2)
            for k in range(4):
                f3[k, r3 : r3 + 8] += shift(xr[b, 12], k)

    with jax.named_scope("zfaces"):
        for tile in range(16):
            rows = slice(8 * tile, 8 * tile + 8)
            one, two = zr[0, 0, rows], zr[0, 1, rows]
            s10 = BETA * one
            d2m = one + GAMMA * (two + s10)
            d20 = GAMMA * s10
            s20 = s10 + DELTA * (d2m + d20)
            out[0, rows] += ZETA * s20
            out[1, rows] += (1 / ZETA) * d20
            out[2, rows] += (ZETA * DELTA) * d20
            one, two = zr[1, 0, rows], zr[1, 1, rows]
            d17 = ALPHA * one
            s17 = BETA * d17
            d27 = d17 + GAMMA * (s17 + two + s17)
            d26 = GAMMA * s17
            s27 = s17 + DELTA * (d26 + d27)
            out[nz - 4, rows] += (ZETA * DELTA) * d26
            out[nz - 3, rows] += (1 / ZETA) * d26
            out[nz - 2, rows] += ZETA * s27
            out[nz - 1, rows] += (1 / ZETA) * d27

    with jax.named_scope("final"):
        lane3 = lax.broadcasted_iota(jnp.int32, (32, 128), 1)
        lane2 = lax.broadcasted_iota(jnp.int32, (64, 128), 1)
        parts = []
        for a in range(2):
            first, second = pr[a, 0:64], pr[a, 64:128]
            parts.append((first, shift(first, 1), second))
            for half in range(2):
                for q in range(2):
                    f3[2 * half + q] += shift(pr[a, 64 + 32 * half : 96 + 32 * half], 2 * q)
            for half in range(2):
                take_far(a, slice(16 * half, 16 * half + 16), dr[a], 2 * half)
        for k in range(8):
            total = f2[k]
            for a in range(2):
                total = add((1, total), *[(float(shares[a][k, r]), parts[a][r]) for r in range(3) if abs(shares[a][k, r]) > 1e-12])
            f2[k] = total
            if k % 2 == 0:
                j = k // 2
                even = pl.ds(0, 32, 2)
                f2[k, even, :] = jnp.where(lane3 % 4 == 0, shift(f3[j], 1), f2[k, even, :])
            even = pl.ds(0, 64, 2)
            out[2 * k, even, :] = jnp.where(lane2 % 2 == 0, f2[k], out[2 * k, even, :])

    with jax.named_scope("sendwait"):
        for copy in copies:
            copy.wait_send()


def local(turbulence, consts, shares, far_share):
    nz, nx, ny = turbulence.shape
    f32 = jnp.float32
    vmem = lambda *shape: pltpu.VMEM(shape, f32)
    pair = lambda *shape: [vmem(*shape), vmem(*shape)]
    count = 20
    return pl.pallas_call(
        functools.partial(kernel, shares, far_share),
        out_shape=jax.ShapeDtypeStruct(turbulence.shape, f32),
        in_specs=[pl.BlockSpec(memory_space=pltpu.HBM)] * (1 + len(consts)),
        out_specs=pl.BlockSpec(memory_space=pltpu.VMEM),
        scratch_shapes=[
            vmem(nz, nx, ny),
            *[pltpu.VMEM(c.shape, c.dtype) for c in consts],
            vmem(nz, nx, 2 * ny), vmem(nz, 136, ny), vmem(nz, 80, ny), vmem(nz, 48, ny),
            vmem(8, 64, ny), vmem(4, 32, ny),
            vmem(nz, 8, ny), vmem(2, 2, 8, ny),
            *pair(2, nz, 8, nx),
            *pair(2, 13, 8, ny),
            *pair(2, 2, nx, ny),
            *pair(2, 8, nx),
            *pair(2, 128, ny),
            *pair(4, 4, 8, ny),
            *pair(2, 16, ny),
            *pair(4, 8, ny),
            pltpu.SemaphoreType.DMA((1 + len(consts),)),
            pltpu.SemaphoreType.DMA((count,)),
            pltpu.SemaphoreType.DMA((count,)),
        ],
        compiler_params=pltpu.CompilerParams(collective_id=0, has_side_effects=True, vmem_limit_bytes=48 << 20),
    )(*[pltpu.with_memory_space_constraint(a, pltpu.HBM) for a in (turbulence, *consts)])


def solution(mesh):
    def run(turbulence):
        nz, n, _ = turbulence.shape
        t = tables(n, n * lax.axis_size("gx"))
        names = ("sa", "wa", "wb", "g1a", "g1b", "g2a", "g2b", "ra")
        along_z = nz, nz * lax.axis_size("gz")
        return local(turbulence, [jnp.asarray(t[k]) for k in names], level2_shares(*along_z), level3_shares(*along_z))

    spec = P(*AXES)
    return jax.shard_map(run, mesh=mesh, in_specs=(spec,), out_specs=spec, check_vma=False)
```

```python
import functools

import jax
import jax.numpy as jnp
import ml_dtypes
import numpy as np
from jax import lax
from jax.experimental import pallas as pl
from jax.experimental.pallas import tpu as pltpu
from jax.sharding import PartitionSpec as P

ALPHA = -1.586134342059924
BETA = -0.052980118572961
GAMMA = 0.882911075530934
DELTA = 0.443506852043971
ZETA = 1.149604398860241
AXES = ("gz", "gx", "gy")
BF16 = ml_dtypes.bfloat16
X_RANKS = (2, 3, 4)


def lifting_matrix(n):
    v = np.eye(n)
    s, d = v[0::2].copy(), v[1::2].copy()
    d = d + ALPHA * (s + np.roll(s, -1, 0))
    s = s + BETA * (np.roll(d, 1, 0) + d)
    d = d + GAMMA * (s + np.roll(s, -1, 0))
    s = s + DELTA * (np.roll(d, 1, 0) + d)
    out = np.zeros((n, n))
    out[0::2], out[1::2] = s * ZETA, d / ZETA
    return out


def blocks(n, total):
    m, k, out = np.eye(total), total, []
    p = total // n // 2
    for level in range(3):
        t = lifting_matrix(k) @ m
        rows = t[p * k * n // total : (p + 1) * k * n // total]
        out.append([rows[:, (p + o) * n : (p + o + 1) * n] for o in (-1, 0, 1)])
        m, k = t[0::2], k // 2
    return out


def split(m):
    hi = m.astype(np.float32).astype(BF16)
    lo = (m - hi.astype(np.float64)).astype(np.float32).astype(BF16)
    return hi, lo


def low_rank(m, first, rank, rank_first):
    v = np.linalg.svd(m[:first])[2][:rank_first]
    rest = np.linalg.svd(m - m @ v.T @ v)[2][: rank - rank_first]
    v = np.concatenate([v, rest])
    left = m @ v.T
    left[:first, rank_first:] = 0
    return left, v


def tables(n, total):
    per_level = blocks(n, total)
    place = np.zeros((2 * n, n + n // 2 + n // 4))
    place[np.arange(n), np.arange(n)] = 1
    place[n + 2 * np.arange(n // 2), n + np.arange(n // 2)] = 1
    place[n + 4 * np.arange(n // 4) + 1, n + n // 2 + np.arange(n // 4)] = 1
    before, own, after = (place @ np.concatenate([lv[o] for lv in per_level]) for o in range(3))
    r_before, s_before = low_rank(before, n, 6, 2)
    r_after, s_after = low_rank(after, n, 6, 2)
    send = np.zeros((16, n))
    send[0:6], send[8:14] = s_before, s_after
    take = np.zeros((16, 2 * n))
    take[0:6], take[8:14] = r_before.T, r_after.T
    w_hi, w_lo = split(own.T)
    t_hi, t_lo = split(take)
    ext = []
    for lv, w, slot, rows in zip(per_level, X_RANKS, (2, 4, 4), (136, 80, 48)):
        m = np.zeros((rows, n))
        own_rows = len(lv[1])
        m[:own_rows] = lv[1]
        m[own_rows : own_rows + w] = lv[0][:w]
        m[own_rows + slot : own_rows + slot + w] = lv[2][-w:]
        ext.append(m)
    g1_hi, g1_lo = split(ext[0])
    g2_hi, g2_lo = split(np.concatenate(ext[1:]))
    return dict(
        sa=np.concatenate(split(send)),
        wa=np.concatenate([w_hi, w_hi]),
        wb=w_lo,
        g1a=np.concatenate([g1_hi, g1_hi], axis=1),
        g1b=g1_lo,
        g2a=np.concatenate([g2_hi, g2_hi], axis=1),
        g2b=g2_lo,
        ra=np.concatenate([t_hi, t_hi, t_lo]),
    )


def x_shares(n, total):
    return [
        (before[:8] @ np.linalg.pinv(before[:w], rcond=1e-9), after[-8:] @ np.linalg.pinv(after[-w:], rcond=1e-9))
        for (before, _, after), w in zip(blocks(n, total), X_RANKS)
    ]


def level2_shares(n, total):
    before, _, after = blocks(n, total)[1]
    return before @ np.linalg.pinv(before[0:3]), after @ np.linalg.pinv(after[5:8])


def level3_shares(n, total):
    m = np.eye(total)
    for k in (total, total // 2, total // 4):
        rows = lifting_matrix(k) @ m
        m = rows[0::2]
    p = total // n // 2
    far = rows[p * n // 4 : (p + 1) * n // 4, (p - 2) * n : (p - 1) * n]
    return (far @ np.linalg.pinv(far[0:2]))[2]


def add(*terms):
    total = None
    for coefficient, v in terms:
        if v is None:
            continue
        v = v if coefficient == 1 else v * coefficient
        total = v if total is None else total + v
    return total


def plus(base, coefficient, one, two):
    pair = one if two is None else two if one is None else one + two
    return add((1, base), (coefficient, pair))


def lift_zero_extended(v, lowest, highest, low_only=False):
    a, b = lowest // 2 - 2, highest // 2 + 3
    s = {i: v.get(2 * i) for i in range(a, b + 1)}
    d = {i: v.get(2 * i + 1) for i in range(a, b + 1)}
    d1 = {i: plus(d[i], ALPHA, s[i], s[i + 1]) for i in range(a, b)}
    s1 = {i: plus(s[i], BETA, d1[i - 1], d1[i]) for i in range(a + 1, b)}
    d2 = {i: plus(d1[i], GAMMA, s1[i], s1[i + 1]) for i in range(a + 1, b - 1)}
    s2 = {i: plus(s1[i], DELTA, d2[i - 1], d2[i]) for i in range(a + 2, b - 1)}
    out = {}
    for i in range(a + 2, b - 1):
        for k, part, scale in ((2 * i, s2[i], ZETA), (2 * i + 1, d2[i], 1 / ZETA)):
            if lowest <= k <= highest and part is not None and not (low_only and k % 2):
                out[k] = part * scale
    return out, d1, s1


def halo_parts(v):
    bf = jnp.bfloat16
    hi = v.astype(bf)
    return hi, (v - hi.astype(jnp.float32)).astype(bf)


def dot(a, b, dims=((1,), (0,))):
    return lax.dot_general(a, b, (dims, ((), ())), preferred_element_type=jnp.float32)


def neighbour(offsets):
    return {
        axis: lax.rem(lax.axis_index(axis) + (o + lax.axis_size(axis)), lax.axis_size(axis))
        for axis, o in zip(AXES, offsets)
        if o
    }


SIDES = (1, -1)
CHUNK = 4
PLANES2 = (*range(8), 8, 9, 10, 12, 13, 14)
PLANES3 = (*range(4), 8, 9, 10, 11, 12, 13, 14, 15, 16, 17, 18, 19)
TARGETS = (
    [(a, b, 0) for a in (2, -2, 1, -1, 0) for b in SIDES]
    + [(a, 0, 0) for a in (2, -2, 1, -1)]
    + [(0, 0, c) for c in SIDES]
)


def kernel(edge_shares, shares, far_share, x_hbm, *refs):
    tables_hbm, out, x, tables_vmem, rest = refs[:8], refs[8], refs[9], refs[10:18], refs[18:]
    (
        yc, q1, qs, w, f2, f3, xc, ec,
        ys, yr, xs, xr, zs, zr, ts, tr, ps, pr, es, er, ds, dr, cs, cr,
        load_sem, send_sem, recv_sem,
    ) = rest
    nz, nx, ny = x.shape
    f32 = jnp.float32

    x_loads = [
        pltpu.make_async_copy(x_hbm.at[CHUNK * k : CHUNK * k + CHUNK], x.at[CHUNK * k : CHUNK * k + CHUNK], load_sem.at[k])
        for k in range(nz // CHUNK)
    ]
    loads = [
        pltpu.make_async_copy(a, b, load_sem.at[k]) for k, (a, b) in enumerate(zip(tables_hbm, tables_vmem), len(x_loads))
    ]
    for load in (*x_loads, loads[0]):
        load.start()
    sa, wa, wb, g1a, g1b, g2a, g2b, ra = tables_vmem
    barrier = pltpu.get_barrier_semaphore()
    for offsets in TARGETS:
        pl.semaphore_signal(barrier, inc=1, device_id=neighbour(offsets), device_id_type=pl.DeviceIdType.MESH)
    for load in loads[1:]:
        load.start()

    copies, p_copy, d_copy, c_copy, e_copy, t_copy, x_copy = [], {}, {}, {}, {}, {}, {}

    def send(source, target, offsets):
        k = len(copies)
        copy = pltpu.make_async_remote_copy(
            source, target, send_sem.at[k], recv_sem.at[k],
            device_id=neighbour(offsets), device_id_type=pl.DeviceIdType.MESH,
        )
        copies.append(copy)
        copy.start()
        return copy

    row = lax.broadcasted_iota(jnp.int32, (8, 128), 0)
    lane = lax.broadcasted_iota(jnp.int32, (8, 128), 1)

    def slots(parts, width, first):
        total = None
        for k, v in enumerate(parts):
            amount = (k * width - first) % 8
            v = pltpu.roll(v, amount, 0) if amount else v
            total = v if total is None else jnp.where(row < k * width, total, v)
        return total

    columns = {}
    for level, sides in enumerate(edge_shares):
        for b, m in enumerate(sides):
            for r in range(m.shape[1]):
                column = jnp.zeros((8, 128), f32)
                for k in range(8):
                    if abs(m[k, r]) > 1e-12:
                        column = jnp.where(row == k, float(m[k, r]), column)
                columns[level, b, r] = column

    def spread(level, b, v, first):
        return sum(columns[level, b, r] * v[first + r : first + r + 1] for r in range(X_RANKS[level]))

    def lane_of(v):
        return lax.broadcasted_iota(jnp.int32, v.shape, 1)

    def pack2(one, two):
        two = jnp.zeros_like(one) if two is None else pltpu.roll(two, 1, 1)
        return jnp.where(lane_of(one) % 2 == 0, one, two)

    def pack4(parts):
        total = parts[0]
        for k, part in enumerate(parts[1:], 1):
            total = jnp.where(lane_of(part) % 4 == (1 + k) % 4, pltpu.roll(part, k, 1), total)
        return total

    def lift_level2(v):
        c2, _, _ = lift_zero_extended(v, -4, nz + 3, True)
        o, _, _ = lift_zero_extended({k // 2: w for k, w in c2.items()}, -3, 10)
        return [o[k] for k in (*range(8), 8, 9, 10, -3, -2, -1)]

    def lift_level3(v):
        c2, _, _ = lift_zero_extended(v, -4, nz + 3, True)
        c3, _, _ = lift_zero_extended({k // 2: w for k, w in c2.items()}, -6, 12, True)
        o, _, _ = lift_zero_extended({k // 2: w for k, w in c3.items()}, -6, 10)
        return [o[k] for k in (*range(4), 4, 5, 6, 7, -4, -3, -2, -1, 8, 9, -6, -5)]

    def shift(v, k):
        return pltpu.roll(v, 128 - k, 1) if k else v

    def lift_level1(v):
        o, d1, s1 = lift_zero_extended(v, 0, nz - 1)
        return o, ((d1[nz // 2 - 1], s1[nz // 2 - 1]), (v[0], v[0] + BETA * d1[0]))

    def expand(h, lanes):
        hi, lo = halo_parts(h)
        return dot(jnp.concatenate([hi, lo, hi], axis=0), ra[:, lanes], ((0,), (0,)))

    level1, deeper = slice(0, 128), slice(128, 256)

    with jax.named_scope("load"):
        loads[0].wait()

    with jax.named_scope("ymsg"):
        for k, load in enumerate(x_loads):
            load.wait()
            hi, lo = halo_parts(x[CHUNK * k : CHUNK * k + CHUNK].reshape(CHUNK * nx, ny))
            first = dot(sa[...], hi, ((1,), (1,)))
            message = first[0:16] + first[16:32] + dot(sa[0:16], lo, ((1,), (1,)))
            for z in range(CHUNK):
                for c in range(2):
                    ys[c, CHUNK * k + z] = message[8 * c : 8 * c + 8, z * nx : (z + 1) * nx]
    with jax.named_scope("barw"):
        for tile in range(16):
            rows = slice(8 * tile, 8 * tile + 8)
            v = {k: x[k, rows] for k in (0, 1, 2, nz - 4, nz - 3, nz - 2, nz - 1)}
            last = v[nz - 1] + ALPHA * v[nz - 2]
            zs[0, 0, rows] = last
            zs[0, 1, rows] = v[nz - 2] + BETA * (v[nz - 3] + ALPHA * (v[nz - 4] + v[nz - 2]) + last)
            zs[1, 0, rows] = v[0]
            zs[1, 1, rows] = v[0] + BETA * (v[1] + ALPHA * (v[0] + v[2]))
        pl.semaphore_wait(barrier, len(TARGETS))
        y_copies = [send(ys.at[k], yr.at[k], (0, 0, c)) for k, c in enumerate(SIDES)]
        z_copies = [send(zs.at[a], zr.at[a], (s, 0, 0)) for a, s in enumerate(SIDES)]

    with jax.named_scope("ycent"):
        for load in loads[1:]:
            load.wait()
        for z in range(nz):
            hi, lo = halo_parts(x[z])
            yc[z] = dot(jnp.concatenate([hi, lo], axis=1), wa[...]) + dot(hi, wb[...])
    with jax.named_scope("x2"):
        for z in range(nz):
            hi, lo = halo_parts(yc[z, :, deeper])
            q = dot(g2a[...], jnp.concatenate([hi, lo], axis=0)) + dot(g2b[...], hi)
            qs[z] = q

    with jax.named_scope("z23"):
        for tile in range(16):
            rows = slice(8 * tile, 8 * tile + 8)
            planes, lift = (PLANES2, lift_level2) if tile < 10 else (PLANES3, lift_level3)
            for k, v in zip(planes, lift({k: qs[k, rows] for k in range(nz)})):
                w[k, rows] = v

    with jax.named_scope("x1"):
        for z in range(nz):
            hi, lo = halo_parts(yc[z, :, level1])
            q1[z] = dot(g1a[...], jnp.concatenate([hi, lo], axis=0)) + dot(g1b[...], hi)
    with jax.named_scope("z1"):
        for tile in range(17):
            rows = slice(8 * tile, 8 * tile + 8)
            o, pairs = lift_level1({k: q1[k, rows] for k in range(nz)})
            for k in range(nz):
                if tile < 16:
                    out[k, rows] = o[k]
                else:
                    xc[k] = o[k]
            if tile == 16:
                for a in range(2):
                    for r in range(2):
                        ec[a, r] = pairs[a][r]

    with jax.named_scope("ywait"):
        for copy in y_copies:
            copy.wait_recv()

    with jax.named_scope("halo"):
        h = jnp.concatenate([yr[0], yr[1]], axis=1).reshape(nz * 16, nx)
        hi, lo = halo_parts(h)
        both = jnp.concatenate([hi, lo], axis=1)
        rhs = ((1,), (1,))
        t1 = (dot(both, g1a[...], rhs) + dot(hi, g1b[...], rhs)).reshape(nz, 16, 136)
        t2 = (dot(both, g2a[...], rhs) + dot(hi, g2b[...], rhs)).reshape(nz, 16, 128)
        t1, t1_pairs = lift_level1({k: t1[k] for k in range(nz)})
        for a in range(2):
            (one, two), (three, four) = ((t[0:8, 0:nx], t[8:16, 0:nx]) for t in t1_pairs[a])
            second, fourth = jnp.where(row < 2, one, pltpu.roll(two, 2, 0)), jnp.where(row < 2, three, pltpu.roll(four, 2, 0))
            ts[a] = jnp.where(row < 4, second, pltpu.roll(fourth, 4, 0))
        from2 = dict(zip(PLANES2, lift_level2({k: t2[k] for k in range(nz)})))
        from3 = dict(zip(PLANES3, lift_level3({k: t2[k] for k in range(nz)})))
        level2_rows = lax.broadcasted_iota(jnp.int32, (16, 128), 1) < 80

    def halo_share(k):
        if k in from2 and k in from3:
            h = jnp.where(level2_rows, from2[k], from3[k])
        elif k in from2:
            h = jnp.where(level2_rows, from2[k], 0.0)
        else:
            h = jnp.where(level2_rows, 0.0, from3[k])
        return expand(h, deeper)

    with jax.named_scope("zplanes"):
        for k in range(8, 20):
            w[k] += halo_share(k)
        edge1 = [[ec[a, r] + expand(t1_pairs[a][r][:, nx : nx + 8], level1) for r in range(2)] for a in range(2)]

    with jax.named_scope("zpack"):
        for a in range(2):
            near = [w.at[8 + 4 * a + k] for k in range(4)]
            ps[a, 0:64] = pack2(near[0][0:64], near[1][0:64])
            odd = [pack2(near[k][80:112], pltpu.roll(near[k + 1][80:112], 1, 1)) for k in (0, 2)]
            odd = [jnp.where(lane_of(v) % 4 == 3, v, near[2 * k][80:112]) for k, v in enumerate(odd)]
            third = near[2][0:64]
            ps[a, 64:128] = jnp.where(lane_of(third) % 2 == 0, third, jnp.concatenate(odd, axis=0))
            far = [w.at[16 + 2 * a + k] for k in range(2)]
            ds[a] = pack4([far[0][80:96], far[1][80:96], far[0][96:112], far[1][96:112]])
            for b in range(2):
                e = 2 * a + b
                near3 = pack4([v[112:120] for v in near])
                far3 = pack4([far[0][112:120], far[1][112:120], far[0][112:120], far[1][112:120]])
                es[e, 0] = jnp.where(row < 4, slots(edge1[a], 2, 2 * b), pltpu.roll(near3, 4 - 4 * b, 0) if b == 0 else near3)
                es[e, 1] = slots([pack2(near[0][64:72], near[1][64:72]), pack2(near[2][64:72], None)], 4, 4 * b)
                cs[e] = slots([far3], 4, 4 * b)
        for a, s in enumerate(SIDES):
            t_copy[a] = send(ts.at[a], tr.at[a], (s, 0, 0))
            d_copy[a] = send(ds.at[a], dr.at[a], (2 * s, 0, 0))
            for b, t in enumerate(SIDES):
                e = 2 * a + b
                c_copy[e] = send(cs.at[e], cr.at[e], (2 * s, t, 0))
                e_copy[e] = send(es.at[e], er.at[e], (s, t, 0))
        for a, s in enumerate(SIDES):
            p_copy[a] = send(ps.at[a], pr.at[a], (s, 0, 0))

    with jax.named_scope("xs"):
        full = [xc[k] + expand(t1[k][:, nx : nx + 8], level1) for k in range(nz)]
        for k in range(nz // 4):
            for b in range(2):
                xs[b, k] = slots(full[4 * k : 4 * k + 4], 2, 2 * b)
        pairs2, thirds = [], []
        for k in range(0, 8, 2):
            one, two = w[k] + halo_share(k), w[k + 1] + halo_share(k + 1)
            f2[k], f2[k + 1] = one[0:64], two[0:64]
            pairs2.append(pack2(one[64:72], two[64:72]))
            if k < 4:
                f3[k], f3[k + 1] = one[80:112], two[80:112]
                thirds += [one[112:120], two[112:120]]
        for b, t in enumerate(SIDES):
            for k in range(2):
                xs[b, 4 + k] = slots(pairs2[2 * k : 2 * k + 2], 4, 4 * b)
            xs[b, 6] = slots([pack4(thirds)], 4, 4 * b)
            x_copy[b] = send(xs.at[b], xr.at[b], (0, t, 0))

    with jax.named_scope("own1"):
        for k in range(nz):
            out[k] += expand(t1[k][:, 0:nx], level1)

    with jax.named_scope("zraw"):
        for copy in z_copies:
            copy.wait_recv()
        for a in range(2):
            for r in range(2):
                hi, lo = halo_parts(zr[a, r])
                y = dot(jnp.concatenate([hi, lo], axis=1), wa[:, level1]) + dot(hi, wb[:, level1])
                hi, lo = halo_parts(y)
                zr[a, r] = dot(g1a[0:nx], jnp.concatenate([hi, lo], axis=0)) + dot(g1b[0:nx], hi)

    def take_far(a, rows, v, first):
        one, two = shift(v, first), shift(v, first + 1)
        if a == 0:
            f3[0, rows] += one
            f3[1, rows] += two
            f3[2, rows] += float(far_share[0]) * one + float(far_share[1]) * two
        else:
            f3[2, rows] += one
            f3[3, rows] += two

    ends = ((0, 0, 0), (nx - 8, nx // 2 - 8, nx // 4 - 8))
    with jax.named_scope("wait_t"):
        for a in range(2):
            t_copy[a].wait_recv()
            for r in range(2):
                quad = pltpu.roll(tr[a], 4, 0) if r else tr[a]
                quad = [jnp.where(row < 2, pltpu.roll(quad, 6, 0) if c else quad, 0.0) for c in range(2)]
                zr[a, r] += expand(jnp.concatenate(quad, axis=0), level1)

    with jax.named_scope("wait_x"):
        for b, (r1, r2, r3) in enumerate(ends):
            x_copy[b].wait_recv()
            for k in range(16):
                out[k, r1 : r1 + 8] += spread(0, b, xr[b, k // 4], 2 * (k % 4))
            for k in range(4):
                pair = spread(1, b, xr[b, 4 + k // 2], 4 * (k % 2))
                for q in range(2):
                    f2[2 * k + q, r2 : r2 + 8] += shift(pair, q)
            quad = spread(2, b, xr[b, 6], 0)
            for k in range(4):
                f3[k, r3 : r3 + 8] += shift(quad, k)

    with jax.named_scope("wait_z"):
        for group in (d_copy, c_copy, e_copy, p_copy):
            for copy in group.values():
                copy.wait_recv()
    with jax.named_scope("edges"):
        for a in range(2):
            for half in range(2):
                take_far(a, slice(16 * half, 16 * half + 16), dr[a], 2 * half)
                for q in range(2):
                    f3[2 * half + q] += shift(pr[a, 64 + 32 * half : 96 + 32 * half], 2 * q)
            for b, (r1, r2, r3) in enumerate(ends):
                e = 2 * a + b
                for r in range(2):
                    zr[a, r, r1 : r1 + 8] += spread(0, b, er[e, 0], 2 * r)
                    pr[a, 64 * r + r2 : 64 * r + r2 + 8] += spread(1, b, er[e, 1], 4 * r)
                quad = spread(2, b, er[e, 0], 4)
                for j in range(4):
                    f3[j, r3 : r3 + 8] += shift(quad, j)
                take_far(a, slice(r3, r3 + 8), spread(2, b, cr[e], 0), 0)

    with jax.named_scope("zfaces"):
        for tile in range(16):
            rows = slice(8 * tile, 8 * tile + 8)
            one, two = zr[0, 0, rows], zr[0, 1, rows]
            s10 = BETA * one
            d2m = one + GAMMA * (two + s10)
            d20 = GAMMA * s10
            s20 = s10 + DELTA * (d2m + d20)
            out[0, rows] += ZETA * s20
            out[1, rows] += (1 / ZETA) * d20
            out[2, rows] += (ZETA * DELTA) * d20
            one, two = zr[1, 0, rows], zr[1, 1, rows]
            d17 = ALPHA * one
            s17 = BETA * d17
            d27 = d17 + GAMMA * (s17 + two + s17)
            d26 = GAMMA * s17
            s27 = s17 + DELTA * (d26 + d27)
            out[nz - 4, rows] += (ZETA * DELTA) * d26
            out[nz - 3, rows] += (1 / ZETA) * d26
            out[nz - 2, rows] += ZETA * s27
            out[nz - 1, rows] += (1 / ZETA) * d27

    with jax.named_scope("final"):
        lane3 = lax.broadcasted_iota(jnp.int32, (32, 128), 1)
        lane2 = lax.broadcasted_iota(jnp.int32, (64, 128), 1)
        parts = []
        for a in range(2):
            first, second = pr[a, 0:64], pr[a, 64:128]
            parts.append((first, shift(first, 1), second))
        for k in range(8):
            total = f2[k]
            for a in range(2):
                total = add((1, total), *[(float(shares[a][k, r]), parts[a][r]) for r in range(3) if abs(shares[a][k, r]) > 1e-12])
            f2[k] = total
            if k % 2 == 0:
                j = k // 2
                even = pl.ds(0, 32, 2)
                f2[k, even, :] = jnp.where(lane3 % 4 == 0, shift(f3[j], 1), f2[k, even, :])
            even = pl.ds(0, 64, 2)
            out[2 * k, even, :] = jnp.where(lane2 % 2 == 0, f2[k], out[2 * k, even, :])

    with jax.named_scope("sendwait"):
        for copy in copies:
            copy.wait_send()


def local(turbulence, consts, edge_shares, shares, far_share):
    nz, nx, ny = turbulence.shape
    f32 = jnp.float32
    vmem = lambda *shape: pltpu.VMEM(shape, f32)
    pair = lambda *shape: [vmem(*shape), vmem(*shape)]
    count = 20
    return pl.pallas_call(
        functools.partial(kernel, edge_shares, shares, far_share),
        out_shape=jax.ShapeDtypeStruct(turbulence.shape, f32),
        in_specs=[pl.BlockSpec(memory_space=pltpu.HBM)] * (1 + len(consts)),
        out_specs=pl.BlockSpec(memory_space=pltpu.VMEM),
        scratch_shapes=[
            vmem(nz, nx, ny),
            *[pltpu.VMEM(c.shape, c.dtype) for c in consts],
            vmem(nz, nx, 2 * ny), vmem(nz, 136, ny), vmem(nz, 128, ny), vmem(20, 128, ny),
            vmem(8, 64, ny), vmem(4, 32, ny),
            vmem(nz, 8, ny), vmem(2, 2, 8, ny),
            *pair(2, nz, 8, nx),
            *pair(2, 7, 8, ny),
            *pair(2, 2, nx, ny),
            *pair(2, 8, nx),
            *pair(2, 128, ny),
            *pair(4, 2, 8, ny),
            *pair(2, 16, ny),
            *pair(4, 8, ny),
            pltpu.SemaphoreType.DMA((nz // CHUNK + len(consts),)),
            pltpu.SemaphoreType.DMA((count,)),
            pltpu.SemaphoreType.DMA((count,)),
        ],
        compiler_params=pltpu.CompilerParams(collective_id=0, has_side_effects=True, vmem_limit_bytes=48 << 20),
    )(*[pltpu.with_memory_space_constraint(a, pltpu.HBM) for a in (turbulence, *consts)])


def solution(mesh):
    def run(turbulence):
        nz, n, _ = turbulence.shape
        t = tables(n, n * lax.axis_size("gx"))
        names = ("sa", "wa", "wb", "g1a", "g1b", "g2a", "g2b", "ra")
        along_x, along_z = (n, n * lax.axis_size("gx")), (nz, nz * lax.axis_size("gz"))
        consts = [jnp.asarray(t[k]) for k in names]
        return local(turbulence, consts, x_shares(*along_x), level2_shares(*along_z), level3_shares(*along_z))

    spec = P(*AXES)
    return jax.shard_map(run, mesh=mesh, in_specs=(spec,), out_specs=spec, check_vma=False)
```

```python
import functools

import jax
import jax.numpy as jnp
import ml_dtypes
import numpy as np
from jax import lax
from jax.experimental import pallas as pl
from jax.experimental.pallas import tpu as pltpu
from jax.sharding import PartitionSpec as P

ALPHA = -1.586134342059924
BETA = -0.052980118572961
GAMMA = 0.882911075530934
DELTA = 0.443506852043971
ZETA = 1.149604398860241
AXES = ("gz", "gx", "gy")
BF16 = ml_dtypes.bfloat16
X_RANKS = (2, 3, 4)


def lifting_matrix(n):
    v = np.eye(n)
    s, d = v[0::2].copy(), v[1::2].copy()
    d = d + ALPHA * (s + np.roll(s, -1, 0))
    s = s + BETA * (np.roll(d, 1, 0) + d)
    d = d + GAMMA * (s + np.roll(s, -1, 0))
    s = s + DELTA * (np.roll(d, 1, 0) + d)
    out = np.zeros((n, n))
    out[0::2], out[1::2] = s * ZETA, d / ZETA
    return out


def blocks(n, total):
    m, k, out = np.eye(total), total, []
    p = total // n // 2
    for level in range(3):
        t = lifting_matrix(k) @ m
        rows = t[p * k * n // total : (p + 1) * k * n // total]
        out.append([rows[:, (p + o) * n : (p + o + 1) * n] for o in (-1, 0, 1)])
        m, k = t[0::2], k // 2
    return out


def split(m):
    hi = m.astype(np.float32).astype(BF16)
    lo = (m - hi.astype(np.float64)).astype(np.float32).astype(BF16)
    return hi, lo


def low_rank(m, first, rank, rank_first):
    v = np.linalg.svd(m[:first])[2][:rank_first]
    rest = np.linalg.svd(m - m @ v.T @ v)[2][: rank - rank_first]
    v = np.concatenate([v, rest])
    left = m @ v.T
    left[:first, rank_first:] = 0
    return left, v


def tables(n, total):
    per_level = blocks(n, total)
    place = np.zeros((2 * n, n + n // 2 + n // 4))
    place[np.arange(n), np.arange(n)] = 1
    place[n + 2 * np.arange(n // 2), n + np.arange(n // 2)] = 1
    place[n + 4 * np.arange(n // 4) + 1, n + n // 2 + np.arange(n // 4)] = 1
    before, own, after = (place @ np.concatenate([lv[o] for lv in per_level]) for o in range(3))
    r_before, s_before = low_rank(before, n, 6, 2)
    r_after, s_after = low_rank(after, n, 6, 2)
    send = np.zeros((16, n))
    send[0:6], send[8:14] = s_before, s_after
    take = np.zeros((16, 2 * n))
    take[0:6], take[8:14] = r_before.T, r_after.T
    w_hi, w_lo = split(own.T)
    t_hi, t_lo = split(take)
    ext = []
    for lv, w, slot, rows in zip(per_level, X_RANKS, (2, 4, 4), (136, 80, 48)):
        m = np.zeros((rows, n))
        own_rows = len(lv[1])
        m[:own_rows] = lv[1]
        m[own_rows : own_rows + w] = lv[0][:w]
        m[own_rows + slot : own_rows + slot + w] = lv[2][-w:]
        ext.append(m)
    g1_hi, g1_lo = split(ext[0])
    g2_hi, g2_lo = split(np.concatenate(ext[1:]))
    return dict(
        sa=np.concatenate(split(send)),
        wa=np.concatenate([w_hi, w_hi]),
        wb=w_lo,
        g1a=np.concatenate([g1_hi, g1_hi], axis=1),
        g1b=g1_lo,
        g2a=np.concatenate([g2_hi, g2_hi], axis=1),
        g2b=g2_lo,
        ra=np.concatenate([t_hi, t_hi, t_lo]),
    )


def x_shares(n, total):
    return [
        (before[:8] @ np.linalg.pinv(before[:w], rcond=1e-9), after[-8:] @ np.linalg.pinv(after[-w:], rcond=1e-9))
        for (before, _, after), w in zip(blocks(n, total), X_RANKS)
    ]


def level2_shares(n, total):
    before, _, after = blocks(n, total)[1]
    return before @ np.linalg.pinv(before[0:3]), after @ np.linalg.pinv(after[5:8])


def level3_shares(n, total):
    m = np.eye(total)
    for k in (total, total // 2, total // 4):
        rows = lifting_matrix(k) @ m
        m = rows[0::2]
    p = total // n // 2
    far = rows[p * n // 4 : (p + 1) * n // 4, (p - 2) * n : (p - 1) * n]
    return (far @ np.linalg.pinv(far[0:2]))[2]


def add(*terms):
    total = None
    for coefficient, v in terms:
        if v is None:
            continue
        v = v if coefficient == 1 else v * coefficient
        total = v if total is None else total + v
    return total


def plus(base, coefficient, one, two):
    pair = one if two is None else two if one is None else one + two
    return add((1, base), (coefficient, pair))


def lift_zero_extended(v, lowest, highest, low_only=False):
    a, b = lowest // 2 - 2, highest // 2 + 3
    s = {i: v.get(2 * i) for i in range(a, b + 1)}
    d = {i: v.get(2 * i + 1) for i in range(a, b + 1)}
    d1 = {i: plus(d[i], ALPHA, s[i], s[i + 1]) for i in range(a, b)}
    s1 = {i: plus(s[i], BETA, d1[i - 1], d1[i]) for i in range(a + 1, b)}
    d2 = {i: plus(d1[i], GAMMA, s1[i], s1[i + 1]) for i in range(a + 1, b - 1)}
    s2 = {i: plus(s1[i], DELTA, d2[i - 1], d2[i]) for i in range(a + 2, b - 1)}
    out = {}
    for i in range(a + 2, b - 1):
        for k, part, scale in ((2 * i, s2[i], ZETA), (2 * i + 1, d2[i], 1 / ZETA)):
            if lowest <= k <= highest and part is not None and not (low_only and k % 2):
                out[k] = part * scale
    return out, d1, s1


def halo_parts(v):
    bf = jnp.bfloat16
    hi = v.astype(bf)
    return hi, (v - hi.astype(jnp.float32)).astype(bf)


def dot(a, b, dims=((1,), (0,))):
    return lax.dot_general(a, b, (dims, ((), ())), preferred_element_type=jnp.float32)


def neighbour(offsets):
    return {
        axis: lax.rem(lax.axis_index(axis) + (o + lax.axis_size(axis)), lax.axis_size(axis))
        for axis, o in zip(AXES, offsets)
        if o
    }


SIDES = (1, -1)
CHUNK = 4
PLANES2 = (*range(8), 8, 9, 10, 12, 13, 14)
PLANES3 = (*range(4), 8, 9, 10, 11, 12, 13, 14, 15, 16, 17, 18, 19)
TARGETS = (
    [(a, b, 0) for a in SIDES for b in SIDES]
    + [(0, b, 0) for b in SIDES]
    + [(a, 0, 0) for a in SIDES]
    + [(0, 0, c) for c in SIDES]
)


def kernel(edge_shares, shares, far_share, x_hbm, *refs):
    tables_hbm, out, x, tables_vmem, rest = refs[:8], refs[8], refs[9], refs[10:18], refs[18:]
    (
        yc, q1, qs, w, f2, f3, xc, ec,
        ys, yr, xs, xr, zs, zr, ts, tr, ps, pr, es, er, ds, dr, cs, cr,
        load_sem, send_sem, recv_sem,
    ) = rest
    nz, nx, ny = x.shape
    f32 = jnp.float32

    x_loads = [
        pltpu.make_async_copy(x_hbm.at[CHUNK * k : CHUNK * k + CHUNK], x.at[CHUNK * k : CHUNK * k + CHUNK], load_sem.at[k])
        for k in range(nz // CHUNK)
    ]
    loads = [
        pltpu.make_async_copy(a, b, load_sem.at[k]) for k, (a, b) in enumerate(zip(tables_hbm, tables_vmem), len(x_loads))
    ]
    for load in (loads[0], *x_loads):
        load.start()
    sa, wa, wb, g1a, g1b, g2a, g2b, ra = tables_vmem
    barrier = pltpu.get_barrier_semaphore()
    for offsets in TARGETS:
        pl.semaphore_signal(barrier, inc=1, device_id=neighbour(offsets), device_id_type=pl.DeviceIdType.MESH)
    for load in loads[1:]:
        load.start()

    copies, p_copy, d_copy, c_copy, e_copy, t_copy, x_copy = [], {}, {}, {}, {}, {}, {}

    def send(source, target, offsets):
        k = len(copies)
        copy = pltpu.make_async_remote_copy(
            source, target, send_sem.at[k], recv_sem.at[k],
            device_id=neighbour(offsets), device_id_type=pl.DeviceIdType.MESH,
        )
        copies.append(copy)
        copy.start()
        return copy

    row = lax.broadcasted_iota(jnp.int32, (8, 128), 0)
    lane = lax.broadcasted_iota(jnp.int32, (8, 128), 1)

    def slots(parts, width, first):
        total = None
        for k, v in enumerate(parts):
            amount = (k * width - first) % 8
            v = pltpu.roll(v, amount, 0) if amount else v
            total = v if total is None else jnp.where(row < k * width, total, v)
        return total

    columns = {}
    for level, sides in enumerate(edge_shares):
        for b, m in enumerate(sides):
            for r in range(m.shape[1]):
                column = jnp.zeros((8, 128), f32)
                for k in range(8):
                    if abs(m[k, r]) > 1e-12:
                        column = jnp.where(row == k, float(m[k, r]), column)
                columns[level, b, r] = column

    def spread(level, b, v, first):
        return sum(columns[level, b, r] * v[first + r : first + r + 1] for r in range(X_RANKS[level]))

    def lane_of(v):
        return lax.broadcasted_iota(jnp.int32, v.shape, 1)

    def pack2(one, two):
        two = jnp.zeros_like(one) if two is None else pltpu.roll(two, 1, 1)
        return jnp.where(lane_of(one) % 2 == 0, one, two)

    def pack4(parts):
        total = parts[0]
        for k, part in enumerate(parts[1:], 1):
            total = jnp.where(lane_of(part) % 4 == (1 + k) % 4, pltpu.roll(part, k, 1), total)
        return total

    def lift_level2(v):
        c2, _, _ = lift_zero_extended(v, -4, nz + 3, True)
        o, _, _ = lift_zero_extended({k // 2: w for k, w in c2.items()}, -3, 10)
        return [o[k] for k in (*range(8), 8, 9, 10, -3, -2, -1)]

    def lift_level3(v):
        c2, _, _ = lift_zero_extended(v, -4, nz + 3, True)
        c3, _, _ = lift_zero_extended({k // 2: w for k, w in c2.items()}, -6, 12, True)
        o, _, _ = lift_zero_extended({k // 2: w for k, w in c3.items()}, -6, 10)
        return [o[k] for k in (*range(4), 4, 5, 6, 7, -4, -3, -2, -1, 8, 9, -6, -5)]

    def shift(v, k):
        return pltpu.roll(v, 128 - k, 1) if k else v

    def lift_level1(v):
        o, d1, s1 = lift_zero_extended(v, 0, nz - 1)
        return o, ((d1[nz // 2 - 1], s1[nz // 2 - 1]), (v[0], v[0] + BETA * d1[0]))

    def expand(h, lanes):
        hi, lo = halo_parts(h)
        return dot(jnp.concatenate([hi, lo, hi], axis=0), ra[:, lanes], ((0,), (0,)))

    level1, deeper = slice(0, 128), slice(128, 256)

    with jax.named_scope("load"):
        loads[0].wait()

    with jax.named_scope("ymsg"):
        for k, load in enumerate(x_loads):
            load.wait()
            hi, lo = halo_parts(x[CHUNK * k : CHUNK * k + CHUNK].reshape(CHUNK * nx, ny))
            first = dot(sa[...], hi, ((1,), (1,)))
            message = first[0:16] + first[16:32] + dot(sa[0:16], lo, ((1,), (1,)))
            for z in range(CHUNK):
                for c in range(2):
                    ys[c, CHUNK * k + z] = message[8 * c : 8 * c + 8, z * nx : (z + 1) * nx]
    with jax.named_scope("barw"):
        for tile in range(16):
            rows = slice(8 * tile, 8 * tile + 8)
            v = {k: x[k, rows] for k in (0, 1, 2, nz - 4, nz - 3, nz - 2, nz - 1)}
            last = v[nz - 1] + ALPHA * v[nz - 2]
            zs[0, 0, rows] = last
            zs[0, 1, rows] = v[nz - 2] + BETA * (v[nz - 3] + ALPHA * (v[nz - 4] + v[nz - 2]) + last)
            zs[1, 0, rows] = v[0]
            zs[1, 1, rows] = v[0] + BETA * (v[1] + ALPHA * (v[0] + v[2]))
        pl.semaphore_wait(barrier, len(TARGETS))
        y_copies = [send(ys.at[k], yr.at[k], (0, 0, c)) for k, c in enumerate(SIDES)]
        z_copies = [send(zs.at[a], zr.at[a], (s, 0, 0)) for a, s in enumerate(SIDES)]

    with jax.named_scope("ycent"):
        for load in loads[1:]:
            load.wait()
        for z in range(nz):
            hi, lo = halo_parts(x[z])
            yc[z] = dot(jnp.concatenate([hi, lo], axis=1), wa[...]) + dot(hi, wb[...])
    with jax.named_scope("x2"):
        for z in range(nz):
            hi, lo = halo_parts(yc[z, :, deeper])
            q = dot(g2a[...], jnp.concatenate([hi, lo], axis=0)) + dot(g2b[...], hi)
            qs[z] = q

    with jax.named_scope("z23"):
        for tile in range(16):
            rows = slice(8 * tile, 8 * tile + 8)
            planes, lift = (PLANES2, lift_level2) if tile < 10 else (PLANES3, lift_level3)
            for k, v in zip(planes, lift({k: qs[k, rows] for k in range(nz)})):
                w[k, rows] = v

    with jax.named_scope("x1"):
        for z in range(nz):
            hi, lo = halo_parts(yc[z, :, level1])
            q1[z] = dot(g1a[...], jnp.concatenate([hi, lo], axis=0)) + dot(g1b[...], hi)
    with jax.named_scope("z1"):
        for tile in range(17):
            rows = slice(8 * tile, 8 * tile + 8)
            o, pairs = lift_level1({k: q1[k, rows] for k in range(nz)})
            for k in range(nz):
                if tile < 16:
                    out[k, rows] = o[k]
                else:
                    xc[k] = o[k]
            if tile == 16:
                for a in range(2):
                    for r in range(2):
                        ec[a, r] = pairs[a][r]

    with jax.named_scope("ywait"):
        for copy in y_copies:
            copy.wait_recv()

    with jax.named_scope("halo"):
        h = jnp.concatenate([yr[0], yr[1]], axis=1).reshape(nz * 16, nx)
        hi, lo = halo_parts(h)
        both = jnp.concatenate([hi, lo], axis=1)
        rhs = ((1,), (1,))
        t2 = (dot(both, g2a[...], rhs) + dot(hi, g2b[...], rhs)).reshape(nz, 16, 128)
        from2 = dict(zip(PLANES2, lift_level2({k: t2[k] for k in range(nz)})))
        from3 = dict(zip(PLANES3, lift_level3({k: t2[k] for k in range(nz)})))
        level2_rows = lax.broadcasted_iota(jnp.int32, (16, 128), 1) < 80

    def halo_share(k):
        if k in from2 and k in from3:
            h = jnp.where(level2_rows, from2[k], from3[k])
        elif k in from2:
            h = jnp.where(level2_rows, from2[k], 0.0)
        else:
            h = jnp.where(level2_rows, 0.0, from3[k])
        return expand(h, deeper)

    with jax.named_scope("zplanes"):
        for k in range(8, 20):
            w[k] += halo_share(k)

    with jax.named_scope("zpack"):
        for a in range(2):
            near = [w.at[8 + 4 * a + k] for k in range(4)]
            ps[a, 0:64] = pack2(near[0][0:64], near[1][0:64])
            odd = [pack2(near[k][80:112], pltpu.roll(near[k + 1][80:112], 1, 1)) for k in (0, 2)]
            odd = [jnp.where(lane_of(v) % 4 == 3, v, near[2 * k][80:112]) for k, v in enumerate(odd)]
            third = near[2][0:64]
            ps[a, 64:128] = jnp.where(lane_of(third) % 2 == 0, third, jnp.concatenate(odd, axis=0))
            far = [w.at[16 + 2 * a + k] for k in range(2)]
            ds[a] = pack4([far[0][80:96], far[1][80:96], far[0][96:112], far[1][96:112]])
        for a, s in enumerate(SIDES):
            p_copy[a] = send(ps.at[a], pr.at[a], (s, 0, 0))

    with jax.named_scope("halo1"):
        t1 = (dot(both, g1a[...], rhs) + dot(hi, g1b[...], rhs)).reshape(nz, 16, 136)
        t1, t1_pairs = lift_level1({k: t1[k] for k in range(nz)})
        for a in range(2):
            (one, two), (three, four) = ((t[0:8, 0:nx], t[8:16, 0:nx]) for t in t1_pairs[a])
            second, fourth = jnp.where(row < 2, one, pltpu.roll(two, 2, 0)), jnp.where(row < 2, three, pltpu.roll(four, 2, 0))
            ts[a] = jnp.where(row < 4, second, pltpu.roll(fourth, 4, 0))
        edge1 = [[ec[a, r] + expand(t1_pairs[a][r][:, nx : nx + 8], level1) for r in range(2)] for a in range(2)]
        for a, s in enumerate(SIDES):
            near, far = [w.at[8 + 4 * a + k] for k in range(4)], [w.at[16 + 2 * a + k] for k in range(2)]
            near3 = pack4([v[112:120] for v in near])
            far3 = pack4([far[0][112:120], far[1][112:120], far[0][112:120], far[1][112:120]])
            for b in range(2):
                e = 2 * a + b
                es[e, 0] = jnp.where(row < 4, slots(edge1[a], 2, 2 * b), pltpu.roll(near3, 4, 0) if b == 0 else near3)
                es[e, 1] = slots([pack2(near[0][64:72], near[1][64:72]), pack2(near[2][64:72], None)], 4, 4 * b)
                cs[e] = slots([far3], 4, 4 * b)
        for a, s in enumerate(SIDES):
            t_copy[a] = send(ts.at[a], tr.at[a], (s, 0, 0))
            for b, t in enumerate(SIDES):
                e_copy[2 * a + b] = send(es.at[2 * a + b], er.at[2 * a + b], (s, t, 0))

    with jax.named_scope("xs"):
        full = [xc[k] + expand(t1[k][:, nx : nx + 8], level1) for k in range(nz)]
        for k in range(nz // 4):
            for b in range(2):
                xs[b, k] = slots(full[4 * k : 4 * k + 4], 2, 2 * b)
        pairs2, thirds = [], []
        for k in range(0, 8, 2):
            one, two = w[k] + halo_share(k), w[k + 1] + halo_share(k + 1)
            f2[k], f2[k + 1] = one[0:64], two[0:64]
            pairs2.append(pack2(one[64:72], two[64:72]))
            if k < 4:
                f3[k], f3[k + 1] = one[80:112], two[80:112]
                thirds += [one[112:120], two[112:120]]
        for b, t in enumerate(SIDES):
            for k in range(2):
                xs[b, 4 + k] = slots(pairs2[2 * k : 2 * k + 2], 4, 4 * b)
            xs[b, 6] = slots([pack4(thirds)], 4, 4 * b)
            x_copy[b] = send(xs.at[b], xr.at[b], (0, t, 0))

    with jax.named_scope("zwait"):
        for copy in z_copies:
            copy.wait_recv()
        for a, s in enumerate(SIDES):
            d_copy[a] = send(ds.at[a], dr.at[a], (2 * s, 0, 0))
        for a, s in enumerate(SIDES):
            for b, t in enumerate(SIDES):
                c_copy[2 * a + b] = send(cs.at[2 * a + b], cr.at[2 * a + b], (2 * s, t, 0))

    with jax.named_scope("own1"):
        for k in range(nz):
            out[k] += expand(t1[k][:, 0:nx], level1)

    with jax.named_scope("zraw"):
        for a in range(2):
            for r in range(2):
                hi, lo = halo_parts(zr[a, r])
                y = dot(jnp.concatenate([hi, lo], axis=1), wa[:, level1]) + dot(hi, wb[:, level1])
                hi, lo = halo_parts(y)
                zr[a, r] = dot(g1a[0:nx], jnp.concatenate([hi, lo], axis=0)) + dot(g1b[0:nx], hi)

    def take_far(a, rows, v, first):
        one, two = shift(v, first), shift(v, first + 1)
        if a == 0:
            f3[0, rows] += one
            f3[1, rows] += two
            f3[2, rows] += float(far_share[0]) * one + float(far_share[1]) * two
        else:
            f3[2, rows] += one
            f3[3, rows] += two

    ends = ((0, 0, 0), (nx - 8, nx // 2 - 8, nx // 4 - 8))
    with jax.named_scope("wait_t"):
        for a in range(2):
            t_copy[a].wait_recv()
            for r in range(2):
                quad = pltpu.roll(tr[a], 4, 0) if r else tr[a]
                quad = [jnp.where(row < 2, pltpu.roll(quad, 6, 0) if c else quad, 0.0) for c in range(2)]
                zr[a, r] += expand(jnp.concatenate(quad, axis=0), level1)

    with jax.named_scope("wait_x"):
        for b, (r1, r2, r3) in enumerate(ends):
            x_copy[b].wait_recv()
            for k in range(16):
                out[k, r1 : r1 + 8] += spread(0, b, xr[b, k // 4], 2 * (k % 4))
            for k in range(4):
                pair = spread(1, b, xr[b, 4 + k // 2], 4 * (k % 2))
                for q in range(2):
                    f2[2 * k + q, r2 : r2 + 8] += shift(pair, q)
            quad = spread(2, b, xr[b, 6], 0)
            for k in range(4):
                f3[k, r3 : r3 + 8] += shift(quad, k)

    with jax.named_scope("wait_z"):
        for group in (d_copy, c_copy, e_copy, p_copy):
            for copy in group.values():
                copy.wait_recv()
    with jax.named_scope("edges"):
        for a in range(2):
            for half in range(2):
                take_far(a, slice(16 * half, 16 * half + 16), dr[a], 2 * half)
                for q in range(2):
                    f3[2 * half + q] += shift(pr[a, 64 + 32 * half : 96 + 32 * half], 2 * q)
            for b, (r1, r2, r3) in enumerate(ends):
                e = 2 * a + b
                for r in range(2):
                    zr[a, r, r1 : r1 + 8] += spread(0, b, er[e, 0], 2 * r)
                    pr[a, 64 * r + r2 : 64 * r + r2 + 8] += spread(1, b, er[e, 1], 4 * r)
                quad = spread(2, b, er[e, 0], 4)
                for j in range(4):
                    f3[j, r3 : r3 + 8] += shift(quad, j)
                take_far(a, slice(r3, r3 + 8), spread(2, b, cr[e], 0), 0)

    with jax.named_scope("zfaces"):
        for tile in range(16):
            rows = slice(8 * tile, 8 * tile + 8)
            one, two = zr[0, 0, rows], zr[0, 1, rows]
            s10 = BETA * one
            d2m = one + GAMMA * (two + s10)
            d20 = GAMMA * s10
            s20 = s10 + DELTA * (d2m + d20)
            out[0, rows] += ZETA * s20
            out[1, rows] += (1 / ZETA) * d20
            out[2, rows] += (ZETA * DELTA) * d20
            one, two = zr[1, 0, rows], zr[1, 1, rows]
            d17 = ALPHA * one
            s17 = BETA * d17
            d27 = d17 + GAMMA * (s17 + two + s17)
            d26 = GAMMA * s17
            s27 = s17 + DELTA * (d26 + d27)
            out[nz - 4, rows] += (ZETA * DELTA) * d26
            out[nz - 3, rows] += (1 / ZETA) * d26
            out[nz - 2, rows] += ZETA * s27
            out[nz - 1, rows] += (1 / ZETA) * d27

    with jax.named_scope("final"):
        lane3 = lax.broadcasted_iota(jnp.int32, (32, 128), 1)
        lane2 = lax.broadcasted_iota(jnp.int32, (64, 128), 1)
        parts = []
        for a in range(2):
            first, second = pr[a, 0:64], pr[a, 64:128]
            parts.append((first, shift(first, 1), second))
        for k in range(8):
            total = f2[k]
            for a in range(2):
                total = add((1, total), *[(float(shares[a][k, r]), parts[a][r]) for r in range(3) if abs(shares[a][k, r]) > 1e-12])
            f2[k] = total
            if k % 2 == 0:
                j = k // 2
                even = pl.ds(0, 32, 2)
                f2[k, even, :] = jnp.where(lane3 % 4 == 0, shift(f3[j], 1), f2[k, even, :])
            even = pl.ds(0, 64, 2)
            out[2 * k, even, :] = jnp.where(lane2 % 2 == 0, f2[k], out[2 * k, even, :])

    with jax.named_scope("sendwait"):
        for copy in copies:
            copy.wait_send()


def local(turbulence, consts, edge_shares, shares, far_share):
    nz, nx, ny = turbulence.shape
    f32 = jnp.float32
    vmem = lambda *shape: pltpu.VMEM(shape, f32)
    pair = lambda *shape: [vmem(*shape), vmem(*shape)]
    count = 20
    return pl.pallas_call(
        functools.partial(kernel, edge_shares, shares, far_share),
        out_shape=jax.ShapeDtypeStruct(turbulence.shape, f32),
        in_specs=[pl.BlockSpec(memory_space=pltpu.HBM)] * (1 + len(consts)),
        out_specs=pl.BlockSpec(memory_space=pltpu.VMEM),
        scratch_shapes=[
            vmem(nz, nx, ny),
            *[pltpu.VMEM(c.shape, c.dtype) for c in consts],
            vmem(nz, nx, 2 * ny), vmem(nz, 136, ny), vmem(nz, 128, ny), vmem(20, 128, ny),
            vmem(8, 64, ny), vmem(4, 32, ny),
            vmem(nz, 8, ny), vmem(2, 2, 8, ny),
            *pair(2, nz, 8, nx),
            *pair(2, 7, 8, ny),
            *pair(2, 2, nx, ny),
            *pair(2, 8, nx),
            *pair(2, 128, ny),
            *pair(4, 2, 8, ny),
            *pair(2, 16, ny),
            *pair(4, 8, ny),
            pltpu.SemaphoreType.DMA((nz // CHUNK + len(consts),)),
            pltpu.SemaphoreType.DMA((count,)),
            pltpu.SemaphoreType.DMA((count,)),
        ],
        compiler_params=pltpu.CompilerParams(collective_id=0, has_side_effects=True, vmem_limit_bytes=48 << 20),
    )(*[pltpu.with_memory_space_constraint(a, pltpu.HBM) for a in (turbulence, *consts)])


def solution(mesh):
    def run(turbulence):
        nz, n, _ = turbulence.shape
        t = tables(n, n * lax.axis_size("gx"))
        names = ("sa", "wa", "wb", "g1a", "g1b", "g2a", "g2b", "ra")
        along_x, along_z = (n, n * lax.axis_size("gx")), (nz, nz * lax.axis_size("gz"))
        consts = [jnp.asarray(t[k]) for k in names]
        return local(turbulence, consts, x_shares(*along_x), level2_shares(*along_z), level3_shares(*along_z))

    spec = P(*AXES)
    return jax.shard_map(run, mesh=mesh, in_specs=(spec,), out_specs=spec, check_vma=False)
```

```python
import functools

import jax
import jax.numpy as jnp
import ml_dtypes
import numpy as np
from jax import lax
from jax.experimental import pallas as pl
from jax.experimental.pallas import tpu as pltpu
from jax.sharding import PartitionSpec as P

ALPHA = -1.586134342059924
BETA = -0.052980118572961
GAMMA = 0.882911075530934
DELTA = 0.443506852043971
ZETA = 1.149604398860241
AXES = ("gz", "gx", "gy")
BF16 = ml_dtypes.bfloat16
X_RANKS = (2, 3, 4)


def lifting_matrix(n):
    v = np.eye(n)
    s, d = v[0::2].copy(), v[1::2].copy()
    d = d + ALPHA * (s + np.roll(s, -1, 0))
    s = s + BETA * (np.roll(d, 1, 0) + d)
    d = d + GAMMA * (s + np.roll(s, -1, 0))
    s = s + DELTA * (np.roll(d, 1, 0) + d)
    out = np.zeros((n, n))
    out[0::2], out[1::2] = s * ZETA, d / ZETA
    return out


def blocks(n, total):
    m, k, out = np.eye(total), total, []
    p = total // n // 2
    for level in range(3):
        t = lifting_matrix(k) @ m
        rows = t[p * k * n // total : (p + 1) * k * n // total]
        out.append([rows[:, (p + o) * n : (p + o + 1) * n] for o in (-1, 0, 1)])
        m, k = t[0::2], k // 2
    return out


def split(m):
    hi = m.astype(np.float32).astype(BF16)
    lo = (m - hi.astype(np.float64)).astype(np.float32).astype(BF16)
    return hi, lo


def low_rank(m, first, rank, rank_first):
    v = np.linalg.svd(m[:first])[2][:rank_first]
    rest = np.linalg.svd(m - m @ v.T @ v)[2][: rank - rank_first]
    v = np.concatenate([v, rest])
    left = m @ v.T
    left[:first, rank_first:] = 0
    return left, v


def tables(n, total):
    per_level = blocks(n, total)
    place = np.zeros((2 * n, n + n // 2 + n // 4))
    place[np.arange(n), np.arange(n)] = 1
    place[n + 2 * np.arange(n // 2), n + np.arange(n // 2)] = 1
    place[n + 4 * np.arange(n // 4) + 1, n + n // 2 + np.arange(n // 4)] = 1
    before, own, after = (place @ np.concatenate([lv[o] for lv in per_level]) for o in range(3))
    r_before, s_before = low_rank(before, n, 6, 2)
    r_after, s_after = low_rank(after, n, 6, 2)
    send = np.zeros((16, n))
    send[0:6], send[8:14] = s_before, s_after
    take = np.zeros((16, 2 * n))
    take[0:6], take[8:14] = r_before.T, r_after.T
    w_hi, w_lo = split(own.T)
    t_hi, t_lo = split(take)
    ext = []
    for lv, w, slot, rows in zip(per_level, X_RANKS, (2, 4, 4), (136, 80, 48)):
        m = np.zeros((rows, n))
        own_rows = len(lv[1])
        m[:own_rows] = lv[1]
        m[own_rows : own_rows + w] = lv[0][:w]
        m[own_rows + slot : own_rows + slot + w] = lv[2][-w:]
        ext.append(m)
    g1_hi, g1_lo = split(ext[0])
    g2_hi, g2_lo = split(np.concatenate(ext[1:]))
    return dict(
        sa=np.concatenate(split(send)),
        wa=np.concatenate([w_hi, w_hi]),
        wb=w_lo,
        g1a=np.concatenate([g1_hi, g1_hi], axis=1),
        g1b=g1_lo,
        g2a=np.concatenate([g2_hi, g2_hi], axis=1),
        g2b=g2_lo,
        ra=np.concatenate([t_hi, t_hi, t_lo]),
    )


def x_shares(n, total):
    return [
        (before[:8] @ np.linalg.pinv(before[:w], rcond=1e-9), after[-8:] @ np.linalg.pinv(after[-w:], rcond=1e-9))
        for (before, _, after), w in zip(blocks(n, total), X_RANKS)
    ]


def level2_shares(n, total):
    before, _, after = blocks(n, total)[1]
    return before @ np.linalg.pinv(before[0:3]), after @ np.linalg.pinv(after[5:8])


def level3_shares(n, total):
    m = np.eye(total)
    for k in (total, total // 2, total // 4):
        rows = lifting_matrix(k) @ m
        m = rows[0::2]
    p = total // n // 2
    far = rows[p * n // 4 : (p + 1) * n // 4, (p - 2) * n : (p - 1) * n]
    return (far @ np.linalg.pinv(far[0:2]))[2]


def add(*terms):
    total = None
    for coefficient, v in terms:
        if v is None:
            continue
        v = v if coefficient == 1 else v * coefficient
        total = v if total is None else total + v
    return total


def plus(base, coefficient, one, two):
    pair = one if two is None else two if one is None else one + two
    return add((1, base), (coefficient, pair))


def lift_zero_extended(v, lowest, highest, low_only=False):
    a, b = lowest // 2 - 2, highest // 2 + 3
    s = {i: v.get(2 * i) for i in range(a, b + 1)}
    d = {i: v.get(2 * i + 1) for i in range(a, b + 1)}
    d1 = {i: plus(d[i], ALPHA, s[i], s[i + 1]) for i in range(a, b)}
    s1 = {i: plus(s[i], BETA, d1[i - 1], d1[i]) for i in range(a + 1, b)}
    d2 = {i: plus(d1[i], GAMMA, s1[i], s1[i + 1]) for i in range(a + 1, b - 1)}
    s2 = {i: plus(s1[i], DELTA, d2[i - 1], d2[i]) for i in range(a + 2, b - 1)}
    out = {}
    for i in range(a + 2, b - 1):
        for k, part, scale in ((2 * i, s2[i], ZETA), (2 * i + 1, d2[i], 1 / ZETA)):
            if lowest <= k <= highest and part is not None and not (low_only and k % 2):
                out[k] = part * scale
    return out, d1, s1


def halo_parts(v):
    bf = jnp.bfloat16
    hi = v.astype(bf)
    return hi, (v - hi.astype(jnp.float32)).astype(bf)


def dot(a, b, dims=((1,), (0,))):
    return lax.dot_general(a, b, (dims, ((), ())), preferred_element_type=jnp.float32)


def neighbour(offsets):
    return {
        axis: lax.rem(lax.axis_index(axis) + (o + lax.axis_size(axis)), lax.axis_size(axis))
        for axis, o in zip(AXES, offsets)
        if o
    }


SIDES = (1, -1)
CHUNK = 4
PLANES2 = (*range(8), 8, 9, 10, 12, 13, 14)
PLANES3 = (*range(4), 8, 9, 10, 11, 12, 13, 14, 15, 16, 17, 18, 19)
TARGETS = [(0, b, 0) for b in SIDES] + [(a, 0, 0) for a in SIDES] + [(0, 0, c) for c in SIDES]


def kernel(edge_shares, shares, far_share, x_hbm, *refs):
    tables_hbm, out, x, tables_vmem, rest = refs[:8], refs[8], refs[9], refs[10:18], refs[18:]
    (
        yc, q1, qs, w, f2, f3, xc, ec,
        ys, yr, xs, xr, zs, zr, ts, tr, ps, pr, es, er, ds, dr, cs, cr,
        load_sem, send_sem, recv_sem, hello_sem,
    ) = rest
    nz, nx, ny = x.shape
    f32 = jnp.float32

    x_loads = [
        pltpu.make_async_copy(x_hbm.at[CHUNK * k : CHUNK * k + CHUNK], x.at[CHUNK * k : CHUNK * k + CHUNK], load_sem.at[k])
        for k in range(nz // CHUNK)
    ]
    loads = [
        pltpu.make_async_copy(a, b, load_sem.at[k]) for k, (a, b) in enumerate(zip(tables_hbm, tables_vmem), len(x_loads))
    ]
    for load in (loads[0], *x_loads):
        load.start()
    sa, wa, wb, g1a, g1b, g2a, g2b, ra = tables_vmem
    barrier = pltpu.get_barrier_semaphore()
    for offsets in TARGETS:
        pl.semaphore_signal(barrier, inc=1, device_id=neighbour(offsets), device_id_type=pl.DeviceIdType.MESH)
    for load in loads[1:]:
        load.start()

    copies, p_copy, d_copy, c_copy, e_copy, t_copy, x_copy = [], {}, {}, {}, {}, {}, {}

    def send(source, target, offsets):
        k = len(copies)
        copy = pltpu.make_async_remote_copy(
            source, target, send_sem.at[k], recv_sem.at[k],
            device_id=neighbour(offsets), device_id_type=pl.DeviceIdType.MESH,
        )
        copies.append(copy)
        copy.start()
        return copy

    row = lax.broadcasted_iota(jnp.int32, (8, 128), 0)
    lane = lax.broadcasted_iota(jnp.int32, (8, 128), 1)

    def slots(parts, width, first):
        total = None
        for k, v in enumerate(parts):
            amount = (k * width - first) % 8
            v = pltpu.roll(v, amount, 0) if amount else v
            total = v if total is None else jnp.where(row < k * width, total, v)
        return total

    columns = {}
    for level, sides in enumerate(edge_shares):
        for b, m in enumerate(sides):
            for r in range(m.shape[1]):
                column = jnp.zeros((8, 128), f32)
                for k in range(8):
                    if abs(m[k, r]) > 1e-12:
                        column = jnp.where(row == k, float(m[k, r]), column)
                columns[level, b, r] = column

    def spread(level, b, v, first):
        return sum(columns[level, b, r] * v[first + r : first + r + 1] for r in range(X_RANKS[level]))

    def lane_of(v):
        return lax.broadcasted_iota(jnp.int32, v.shape, 1)

    def pack2(one, two):
        two = jnp.zeros_like(one) if two is None else pltpu.roll(two, 1, 1)
        return jnp.where(lane_of(one) % 2 == 0, one, two)

    def pack4(parts):
        total = parts[0]
        for k, part in enumerate(parts[1:], 1):
            total = jnp.where(lane_of(part) % 4 == (1 + k) % 4, pltpu.roll(part, k, 1), total)
        return total

    def lift_level2(v):
        c2, _, _ = lift_zero_extended(v, -4, nz + 3, True)
        o, _, _ = lift_zero_extended({k // 2: w for k, w in c2.items()}, -3, 10)
        return [o[k] for k in (*range(8), 8, 9, 10, -3, -2, -1)]

    def lift_level3(v):
        c2, _, _ = lift_zero_extended(v, -4, nz + 3, True)
        c3, _, _ = lift_zero_extended({k // 2: w for k, w in c2.items()}, -6, 12, True)
        o, _, _ = lift_zero_extended({k // 2: w for k, w in c3.items()}, -6, 10)
        return [o[k] for k in (*range(4), 4, 5, 6, 7, -4, -3, -2, -1, 8, 9, -6, -5)]

    def shift(v, k):
        return pltpu.roll(v, 128 - k, 1) if k else v

    def lift_level1(v):
        o, d1, s1 = lift_zero_extended(v, 0, nz - 1)
        return o, ((d1[nz // 2 - 1], s1[nz // 2 - 1]), (v[0], v[0] + BETA * d1[0]))

    def expand(h, lanes):
        hi, lo = halo_parts(h)
        return dot(jnp.concatenate([hi, lo, hi], axis=0), ra[:, lanes], ((0,), (0,)))

    level1, deeper = slice(0, 128), slice(128, 256)

    with jax.named_scope("load"):
        loads[0].wait()

    with jax.named_scope("ymsg"):
        for k, load in enumerate(x_loads):
            load.wait()
            hi, lo = halo_parts(x[CHUNK * k : CHUNK * k + CHUNK].reshape(CHUNK * nx, ny))
            first = dot(sa[...], hi, ((1,), (1,)))
            message = first[0:16] + first[16:32] + dot(sa[0:16], lo, ((1,), (1,)))
            for z in range(CHUNK):
                for c in range(2):
                    ys[c, CHUNK * k + z] = message[8 * c : 8 * c + 8, z * nx : (z + 1) * nx]
    with jax.named_scope("barw"):
        for tile in range(16):
            rows = slice(8 * tile, 8 * tile + 8)
            v = {k: x[k, rows] for k in (0, 1, 2, nz - 4, nz - 3, nz - 2, nz - 1)}
            last = v[nz - 1] + ALPHA * v[nz - 2]
            zs[0, 0, rows] = last
            zs[0, 1, rows] = v[nz - 2] + BETA * (v[nz - 3] + ALPHA * (v[nz - 4] + v[nz - 2]) + last)
            zs[1, 0, rows] = v[0]
            zs[1, 1, rows] = v[0] + BETA * (v[1] + ALPHA * (v[0] + v[2]))
        pl.semaphore_wait(barrier, len(TARGETS))
        y_copies = [send(ys.at[k], yr.at[k], (0, 0, c)) for k, c in enumerate(SIDES)]
        z_copies = [send(zs.at[a], zr.at[a], (s, 0, 0)) for a, s in enumerate(SIDES)]

    def hello(first, directions):
        for k, offsets in enumerate(directions):
            pl.semaphore_signal(
                hello_sem.at[first + k], inc=1, device_id=neighbour(offsets), device_id_type=pl.DeviceIdType.MESH
            )

    hello(0, [(a, 0, 0) for a in SIDES])

    with jax.named_scope("ycent"):
        for load in loads[1:]:
            load.wait()
        for z in range(nz):
            hi, lo = halo_parts(x[z])
            yc[z] = dot(jnp.concatenate([hi, lo], axis=1), wa[...]) + dot(hi, wb[...])
    with jax.named_scope("x2"):
        for z in range(nz):
            hi, lo = halo_parts(yc[z, :, deeper])
            q = dot(g2a[...], jnp.concatenate([hi, lo], axis=0)) + dot(g2b[...], hi)
            qs[z] = q

    with jax.named_scope("z23"):
        for tile in range(16):
            rows = slice(8 * tile, 8 * tile + 8)
            planes, lift = (PLANES2, lift_level2) if tile < 10 else (PLANES3, lift_level3)
            for k, v in zip(planes, lift({k: qs[k, rows] for k in range(nz)})):
                w[k, rows] = v

    for k in range(2):
        pl.semaphore_wait(hello_sem.at[k], 1)
    hello(2, [(0, b, 0) for b in SIDES])
    with jax.named_scope("x1"):
        for z in range(nz):
            hi, lo = halo_parts(yc[z, :, level1])
            q1[z] = dot(g1a[...], jnp.concatenate([hi, lo], axis=0)) + dot(g1b[...], hi)
    with jax.named_scope("z1"):
        for tile in range(17):
            rows = slice(8 * tile, 8 * tile + 8)
            o, pairs = lift_level1({k: q1[k, rows] for k in range(nz)})
            for k in range(nz):
                if tile < 16:
                    out[k, rows] = o[k]
                else:
                    xc[k] = o[k]
            if tile == 16:
                for a in range(2):
                    for r in range(2):
                        ec[a, r] = pairs[a][r]

    with jax.named_scope("ywait"):
        for copy in y_copies:
            copy.wait_recv()

    with jax.named_scope("halo"):
        h = jnp.concatenate([yr[0], yr[1]], axis=1).reshape(nz * 16, nx)
        hi, lo = halo_parts(h)
        both = jnp.concatenate([hi, lo], axis=1)
        rhs = ((1,), (1,))
        t2 = (dot(both, g2a[...], rhs) + dot(hi, g2b[...], rhs)).reshape(nz, 16, 128)
        from2 = dict(zip(PLANES2, lift_level2({k: t2[k] for k in range(nz)})))
        from3 = dict(zip(PLANES3, lift_level3({k: t2[k] for k in range(nz)})))
        level2_rows = lax.broadcasted_iota(jnp.int32, (16, 128), 1) < 80

    def halo_share(k):
        if k in from2 and k in from3:
            h = jnp.where(level2_rows, from2[k], from3[k])
        elif k in from2:
            h = jnp.where(level2_rows, from2[k], 0.0)
        else:
            h = jnp.where(level2_rows, 0.0, from3[k])
        return expand(h, deeper)

    with jax.named_scope("zplanes"):
        for k in range(8, 20):
            w[k] += halo_share(k)

    with jax.named_scope("zpack"):
        for a in range(2):
            near = [w.at[8 + 4 * a + k] for k in range(4)]
            ps[a, 0:64] = pack2(near[0][0:64], near[1][0:64])
            odd = [pack2(near[k][80:112], pltpu.roll(near[k + 1][80:112], 1, 1)) for k in (0, 2)]
            odd = [jnp.where(lane_of(v) % 4 == 3, v, near[2 * k][80:112]) for k, v in enumerate(odd)]
            third = near[2][0:64]
            ps[a, 64:128] = jnp.where(lane_of(third) % 2 == 0, third, jnp.concatenate(odd, axis=0))
            far = [w.at[16 + 2 * a + k] for k in range(2)]
            ds[a] = pack4([far[0][80:96], far[1][80:96], far[0][96:112], far[1][96:112]])
        for a, s in enumerate(SIDES):
            d_copy[a] = send(ds.at[a], dr.at[a], (2 * s, 0, 0))
        for a, s in enumerate(SIDES):
            p_copy[a] = send(ps.at[a], pr.at[a], (s, 0, 0))

    with jax.named_scope("halo1"):
        t1 = (dot(both, g1a[...], rhs) + dot(hi, g1b[...], rhs)).reshape(nz, 16, 136)
        t1, t1_pairs = lift_level1({k: t1[k] for k in range(nz)})
        for a in range(2):
            (one, two), (three, four) = ((t[0:8, 0:nx], t[8:16, 0:nx]) for t in t1_pairs[a])
            second, fourth = jnp.where(row < 2, one, pltpu.roll(two, 2, 0)), jnp.where(row < 2, three, pltpu.roll(four, 2, 0))
            ts[a] = jnp.where(row < 4, second, pltpu.roll(fourth, 4, 0))
        edge1 = [[ec[a, r] + expand(t1_pairs[a][r][:, nx : nx + 8], level1) for r in range(2)] for a in range(2)]
        for a, s in enumerate(SIDES):
            near, far = [w.at[8 + 4 * a + k] for k in range(4)], [w.at[16 + 2 * a + k] for k in range(2)]
            near3 = pack4([v[112:120] for v in near])
            far3 = pack4([far[0][112:120], far[1][112:120], far[0][112:120], far[1][112:120]])
            for b in range(2):
                e = 2 * a + b
                es[e, 0] = jnp.where(row < 4, slots(edge1[a], 2, 2 * b), pltpu.roll(near3, 4, 0) if b == 0 else near3)
                es[e, 1] = slots([pack2(near[0][64:72], near[1][64:72]), pack2(near[2][64:72], None)], 4, 4 * b)
                cs[e] = slots([far3], 4, 4 * b)
        for k in (2, 3):
            pl.semaphore_wait(hello_sem.at[k], 1)
        for a, s in enumerate(SIDES):
            for b, t in enumerate(SIDES):
                c_copy[2 * a + b] = send(cs.at[2 * a + b], cr.at[2 * a + b], (2 * s, t, 0))
        for a, s in enumerate(SIDES):
            t_copy[a] = send(ts.at[a], tr.at[a], (s, 0, 0))
            for b, t in enumerate(SIDES):
                e_copy[2 * a + b] = send(es.at[2 * a + b], er.at[2 * a + b], (s, t, 0))

    with jax.named_scope("xs"):
        full = [xc[k] + expand(t1[k][:, nx : nx + 8], level1) for k in range(nz)]
        for k in range(nz // 4):
            for b in range(2):
                xs[b, k] = slots(full[4 * k : 4 * k + 4], 2, 2 * b)
        pairs2, thirds = [], []
        for k in range(0, 8, 2):
            one, two = w[k] + halo_share(k), w[k + 1] + halo_share(k + 1)
            f2[k], f2[k + 1] = one[0:64], two[0:64]
            pairs2.append(pack2(one[64:72], two[64:72]))
            if k < 4:
                f3[k], f3[k + 1] = one[80:112], two[80:112]
                thirds += [one[112:120], two[112:120]]
        for b, t in enumerate(SIDES):
            for k in range(2):
                xs[b, 4 + k] = slots(pairs2[2 * k : 2 * k + 2], 4, 4 * b)
            xs[b, 6] = slots([pack4(thirds)], 4, 4 * b)
            x_copy[b] = send(xs.at[b], xr.at[b], (0, t, 0))

    with jax.named_scope("zwait"):
        for copy in z_copies:
            copy.wait_recv()

    with jax.named_scope("own1"):
        for k in range(nz):
            out[k] += expand(t1[k][:, 0:nx], level1)

    with jax.named_scope("zraw"):
        for a in range(2):
            for r in range(2):
                hi, lo = halo_parts(zr[a, r])
                y = dot(jnp.concatenate([hi, lo], axis=1), wa[:, level1]) + dot(hi, wb[:, level1])
                hi, lo = halo_parts(y)
                zr[a, r] = dot(g1a[0:nx], jnp.concatenate([hi, lo], axis=0)) + dot(g1b[0:nx], hi)

    def take_far(a, rows, v, first):
        one, two = shift(v, first), shift(v, first + 1)
        if a == 0:
            f3[0, rows] += one
            f3[1, rows] += two
            f3[2, rows] += float(far_share[0]) * one + float(far_share[1]) * two
        else:
            f3[2, rows] += one
            f3[3, rows] += two

    ends = ((0, 0, 0), (nx - 8, nx // 2 - 8, nx // 4 - 8))
    with jax.named_scope("wait_t"):
        for a in range(2):
            t_copy[a].wait_recv()
            for r in range(2):
                quad = pltpu.roll(tr[a], 4, 0) if r else tr[a]
                quad = [jnp.where(row < 2, pltpu.roll(quad, 6, 0) if c else quad, 0.0) for c in range(2)]
                zr[a, r] += expand(jnp.concatenate(quad, axis=0), level1)

    with jax.named_scope("wait_x"):
        for b, (r1, r2, r3) in enumerate(ends):
            x_copy[b].wait_recv()
            for k in range(16):
                out[k, r1 : r1 + 8] += spread(0, b, xr[b, k // 4], 2 * (k % 4))
            for k in range(4):
                pair = spread(1, b, xr[b, 4 + k // 2], 4 * (k % 2))
                for q in range(2):
                    f2[2 * k + q, r2 : r2 + 8] += shift(pair, q)
            quad = spread(2, b, xr[b, 6], 0)
            for k in range(4):
                f3[k, r3 : r3 + 8] += shift(quad, k)

    with jax.named_scope("wait_z"):
        for group in (d_copy, c_copy, e_copy, p_copy):
            for copy in group.values():
                copy.wait_recv()
    with jax.named_scope("edges"):
        for a in range(2):
            for half in range(2):
                take_far(a, slice(16 * half, 16 * half + 16), dr[a], 2 * half)
                for q in range(2):
                    f3[2 * half + q] += shift(pr[a, 64 + 32 * half : 96 + 32 * half], 2 * q)
            for b, (r1, r2, r3) in enumerate(ends):
                e = 2 * a + b
                for r in range(2):
                    zr[a, r, r1 : r1 + 8] += spread(0, b, er[e, 0], 2 * r)
                    pr[a, 64 * r + r2 : 64 * r + r2 + 8] += spread(1, b, er[e, 1], 4 * r)
                quad = spread(2, b, er[e, 0], 4)
                for j in range(4):
                    f3[j, r3 : r3 + 8] += shift(quad, j)
                take_far(a, slice(r3, r3 + 8), spread(2, b, cr[e], 0), 0)

    with jax.named_scope("zfaces"):
        for tile in range(16):
            rows = slice(8 * tile, 8 * tile + 8)
            one, two = zr[0, 0, rows], zr[0, 1, rows]
            s10 = BETA * one
            d2m = one + GAMMA * (two + s10)
            d20 = GAMMA * s10
            s20 = s10 + DELTA * (d2m + d20)
            out[0, rows] += ZETA * s20
            out[1, rows] += (1 / ZETA) * d20
            out[2, rows] += (ZETA * DELTA) * d20
            one, two = zr[1, 0, rows], zr[1, 1, rows]
            d17 = ALPHA * one
            s17 = BETA * d17
            d27 = d17 + GAMMA * (s17 + two + s17)
            d26 = GAMMA * s17
            s27 = s17 + DELTA * (d26 + d27)
            out[nz - 4, rows] += (ZETA * DELTA) * d26
            out[nz - 3, rows] += (1 / ZETA) * d26
            out[nz - 2, rows] += ZETA * s27
            out[nz - 1, rows] += (1 / ZETA) * d27

    with jax.named_scope("final"):
        lane3 = lax.broadcasted_iota(jnp.int32, (32, 128), 1)
        lane2 = lax.broadcasted_iota(jnp.int32, (64, 128), 1)
        parts = []
        for a in range(2):
            first, second = pr[a, 0:64], pr[a, 64:128]
            parts.append((first, shift(first, 1), second))
        for k in range(8):
            total = f2[k]
            for a in range(2):
                total = add((1, total), *[(float(shares[a][k, r]), parts[a][r]) for r in range(3) if abs(shares[a][k, r]) > 1e-12])
            f2[k] = total
            if k % 2 == 0:
                j = k // 2
                even = pl.ds(0, 32, 2)
                f2[k, even, :] = jnp.where(lane3 % 4 == 0, shift(f3[j], 1), f2[k, even, :])
            even = pl.ds(0, 64, 2)
            out[2 * k, even, :] = jnp.where(lane2 % 2 == 0, f2[k], out[2 * k, even, :])

    with jax.named_scope("sendwait"):
        for copy in copies:
            copy.wait_send()


def local(turbulence, consts, edge_shares, shares, far_share):
    nz, nx, ny = turbulence.shape
    f32 = jnp.float32
    vmem = lambda *shape: pltpu.VMEM(shape, f32)
    pair = lambda *shape: [vmem(*shape), vmem(*shape)]
    count = 20
    return pl.pallas_call(
        functools.partial(kernel, edge_shares, shares, far_share),
        out_shape=jax.ShapeDtypeStruct(turbulence.shape, f32),
        in_specs=[pl.BlockSpec(memory_space=pltpu.HBM)] * (1 + len(consts)),
        out_specs=pl.BlockSpec(memory_space=pltpu.VMEM),
        scratch_shapes=[
            vmem(nz, nx, ny),
            *[pltpu.VMEM(c.shape, c.dtype) for c in consts],
            vmem(nz, nx, 2 * ny), vmem(nz, 136, ny), vmem(nz, 128, ny), vmem(20, 128, ny),
            vmem(8, 64, ny), vmem(4, 32, ny),
            vmem(nz, 8, ny), vmem(2, 2, 8, ny),
            *pair(2, nz, 8, nx),
            *pair(2, 7, 8, ny),
            *pair(2, 2, nx, ny),
            *pair(2, 8, nx),
            *pair(2, 128, ny),
            *pair(4, 2, 8, ny),
            *pair(2, 16, ny),
            *pair(4, 8, ny),
            pltpu.SemaphoreType.DMA((nz // CHUNK + len(consts),)),
            pltpu.SemaphoreType.DMA((count,)),
            pltpu.SemaphoreType.DMA((count,)),
            pltpu.SemaphoreType.REGULAR((4,)),
        ],
        compiler_params=pltpu.CompilerParams(collective_id=0, has_side_effects=True, vmem_limit_bytes=48 << 20),
    )(*[pltpu.with_memory_space_constraint(a, pltpu.HBM) for a in (turbulence, *consts)])


def solution(mesh):
    def run(turbulence):
        nz, n, _ = turbulence.shape
        t = tables(n, n * lax.axis_size("gx"))
        names = ("sa", "wa", "wb", "g1a", "g1b", "g2a", "g2b", "ra")
        along_x, along_z = (n, n * lax.axis_size("gx")), (nz, nz * lax.axis_size("gz"))
        consts = [jnp.asarray(t[k]) for k in names]
        return local(turbulence, consts, x_shares(*along_x), level2_shares(*along_z), level3_shares(*along_z))

    spec = P(*AXES)
    return jax.shard_map(run, mesh=mesh, in_specs=(spec,), out_specs=spec, check_vma=False)
```

```python
import functools

import jax
import jax.numpy as jnp
import ml_dtypes
import numpy as np
from jax import lax
from jax.experimental import pallas as pl
from jax.experimental.pallas import tpu as pltpu
from jax.sharding import PartitionSpec as P

ALPHA = -1.586134342059924
BETA = -0.052980118572961
GAMMA = 0.882911075530934
DELTA = 0.443506852043971
ZETA = 1.149604398860241
AXES = ("gz", "gx", "gy")
BF16 = ml_dtypes.bfloat16
X_RANKS = (2, 3, 4)


def lifting_matrix(n):
    v = np.eye(n)
    s, d = v[0::2].copy(), v[1::2].copy()
    d = d + ALPHA * (s + np.roll(s, -1, 0))
    s = s + BETA * (np.roll(d, 1, 0) + d)
    d = d + GAMMA * (s + np.roll(s, -1, 0))
    s = s + DELTA * (np.roll(d, 1, 0) + d)
    out = np.zeros((n, n))
    out[0::2], out[1::2] = s * ZETA, d / ZETA
    return out


def blocks(n, total):
    m, k, out = np.eye(total), total, []
    p = total // n // 2
    for level in range(3):
        t = lifting_matrix(k) @ m
        rows = t[p * k * n // total : (p + 1) * k * n // total]
        out.append([rows[:, (p + o) * n : (p + o + 1) * n] for o in (-1, 0, 1)])
        m, k = t[0::2], k // 2
    return out


def split(m):
    hi = m.astype(np.float32).astype(BF16)
    lo = (m - hi.astype(np.float64)).astype(np.float32).astype(BF16)
    return hi, lo


def low_rank(m, first, rank, rank_first):
    v = np.linalg.svd(m[:first])[2][:rank_first]
    rest = np.linalg.svd(m - m @ v.T @ v)[2][: rank - rank_first]
    v = np.concatenate([v, rest])
    left = m @ v.T
    left[:first, rank_first:] = 0
    return left, v


def tables(n, total):
    per_level = blocks(n, total)
    place = np.zeros((2 * n, n + n // 2 + n // 4))
    place[np.arange(n), np.arange(n)] = 1
    place[n + 2 * np.arange(n // 2), n + np.arange(n // 2)] = 1
    place[n + 4 * np.arange(n // 4) + 1, n + n // 2 + np.arange(n // 4)] = 1
    before, own, after = (place @ np.concatenate([lv[o] for lv in per_level]) for o in range(3))
    r_before, s_before = low_rank(before, n, 6, 2)
    r_after, s_after = low_rank(after, n, 6, 2)
    send = np.zeros((16, n))
    send[0:6], send[8:14] = s_before, s_after
    take = np.zeros((16, 2 * n))
    take[0:6], take[8:14] = r_before.T, r_after.T
    w_hi, w_lo = split(own.T)
    t_hi, t_lo = split(take)
    ext = []
    for lv, w, slot, rows in zip(per_level, X_RANKS, (2, 4, 4), (136, 80, 48)):
        m = np.zeros((rows, n))
        own_rows = len(lv[1])
        m[:own_rows] = lv[1]
        m[own_rows : own_rows + w] = lv[0][:w]
        m[own_rows + slot : own_rows + slot + w] = lv[2][-w:]
        ext.append(m)
    g1_hi, g1_lo = split(ext[0])
    g2_hi, g2_lo = split(np.concatenate(ext[1:]))
    return dict(
        sa=np.concatenate(split(send)),
        wa=np.concatenate([w_hi, w_hi]),
        wb=w_lo,
        g1a=np.concatenate([g1_hi, g1_hi], axis=1),
        g1b=g1_lo,
        g2a=np.concatenate([g2_hi, g2_hi], axis=1),
        g2b=g2_lo,
        ra=np.concatenate([t_hi, t_hi, t_lo]),
    )


def x_shares(n, total):
    return [
        (before[:8] @ np.linalg.pinv(before[:w], rcond=1e-9), after[-8:] @ np.linalg.pinv(after[-w:], rcond=1e-9))
        for (before, _, after), w in zip(blocks(n, total), X_RANKS)
    ]


def level2_shares(n, total):
    before, _, after = blocks(n, total)[1]
    return before @ np.linalg.pinv(before[0:3]), after @ np.linalg.pinv(after[5:8])


def level3_shares(n, total):
    m = np.eye(total)
    for k in (total, total // 2, total // 4):
        rows = lifting_matrix(k) @ m
        m = rows[0::2]
    p = total // n // 2
    far = rows[p * n // 4 : (p + 1) * n // 4, (p - 2) * n : (p - 1) * n]
    return (far @ np.linalg.pinv(far[0:2]))[2]


def add(*terms):
    total = None
    for coefficient, v in terms:
        if v is None:
            continue
        v = v if coefficient == 1 else v * coefficient
        total = v if total is None else total + v
    return total


def plus(base, coefficient, one, two):
    pair = one if two is None else two if one is None else one + two
    return add((1, base), (coefficient, pair))


def lift_zero_extended(v, lowest, highest, low_only=False):
    a, b = lowest // 2 - 2, highest // 2 + 3
    s = {i: v.get(2 * i) for i in range(a, b + 1)}
    d = {i: v.get(2 * i + 1) for i in range(a, b + 1)}
    d1 = {i: plus(d[i], ALPHA, s[i], s[i + 1]) for i in range(a, b)}
    s1 = {i: plus(s[i], BETA, d1[i - 1], d1[i]) for i in range(a + 1, b)}
    d2 = {i: plus(d1[i], GAMMA, s1[i], s1[i + 1]) for i in range(a + 1, b - 1)}
    s2 = {i: plus(s1[i], DELTA, d2[i - 1], d2[i]) for i in range(a + 2, b - 1)}
    out = {}
    for i in range(a + 2, b - 1):
        for k, part, scale in ((2 * i, s2[i], ZETA), (2 * i + 1, d2[i], 1 / ZETA)):
            if lowest <= k <= highest and part is not None and not (low_only and k % 2):
                out[k] = part * scale
    return out, d1, s1


def halo_parts(v):
    bf = jnp.bfloat16
    hi = v.astype(bf)
    return hi, (v - hi.astype(jnp.float32)).astype(bf)


def dot(a, b, dims=((1,), (0,))):
    return lax.dot_general(a, b, (dims, ((), ())), preferred_element_type=jnp.float32)


def neighbour(offsets):
    return {
        axis: lax.rem(lax.axis_index(axis) + (o + lax.axis_size(axis)), lax.axis_size(axis))
        for axis, o in zip(AXES, offsets)
        if o
    }


SIDES = (1, -1)
CHUNK = 2
PLANES2 = (*range(8), 8, 9, 10, 12, 13, 14)
PLANES3 = (*range(4), 8, 9, 10, 11, 12, 13, 14, 15, 16, 17, 18, 19)
TARGETS = [(0, b, 0) for b in SIDES] + [(a, 0, 0) for a in SIDES] + [(0, 0, c) for c in SIDES]


def kernel(edge_shares, shares, far_share, x_hbm, *refs):
    tables_hbm, out, x, tables_vmem, rest = refs[:8], refs[8], refs[9], refs[10:18], refs[18:]
    (
        yc, q1, qs, w, f2, f3, xc, ec,
        ys, yr, xs, xr, zs, zr, ts, tr, ps, pr, es, er, ds, dr, cs, cr,
        load_sem, send_sem, recv_sem, hello_sem,
    ) = rest
    nz, nx, ny = x.shape
    f32 = jnp.float32

    x_loads = [
        pltpu.make_async_copy(x_hbm.at[CHUNK * k : CHUNK * k + CHUNK], x.at[CHUNK * k : CHUNK * k + CHUNK], load_sem.at[k])
        for k in range(nz // CHUNK)
    ]
    loads = [
        pltpu.make_async_copy(a, b, load_sem.at[k]) for k, (a, b) in enumerate(zip(tables_hbm, tables_vmem), len(x_loads))
    ]
    for load in (loads[0], *x_loads):
        load.start()
    sa, wa, wb, g1a, g1b, g2a, g2b, ra = tables_vmem
    barrier = pltpu.get_barrier_semaphore()
    for offsets in TARGETS:
        pl.semaphore_signal(barrier, inc=1, device_id=neighbour(offsets), device_id_type=pl.DeviceIdType.MESH)
    for load in loads[1:]:
        load.start()

    copies, p_copy, d_copy, c_copy, e_copy, t_copy, x_copy = [], {}, {}, {}, {}, {}, {}

    def send(source, target, offsets):
        k = len(copies)
        copy = pltpu.make_async_remote_copy(
            source, target, send_sem.at[k], recv_sem.at[k],
            device_id=neighbour(offsets), device_id_type=pl.DeviceIdType.MESH,
        )
        copies.append(copy)
        copy.start()
        return copy

    row = lax.broadcasted_iota(jnp.int32, (8, 128), 0)
    lane = lax.broadcasted_iota(jnp.int32, (8, 128), 1)

    def slots(parts, width, first):
        total = None
        for k, v in enumerate(parts):
            amount = (k * width - first) % 8
            v = pltpu.roll(v, amount, 0) if amount else v
            total = v if total is None else jnp.where(row < k * width, total, v)
        return total

    columns = {}
    for level, sides in enumerate(edge_shares):
        for b, m in enumerate(sides):
            for r in range(m.shape[1]):
                column = jnp.zeros((8, 128), f32)
                for k in range(8):
                    if abs(m[k, r]) > 1e-12:
                        column = jnp.where(row == k, float(m[k, r]), column)
                columns[level, b, r] = column

    def spread(level, b, v, first):
        return sum(columns[level, b, r] * v[first + r : first + r + 1] for r in range(X_RANKS[level]))

    def lane_of(v):
        return lax.broadcasted_iota(jnp.int32, v.shape, 1)

    def pack2(one, two):
        two = jnp.zeros_like(one) if two is None else pltpu.roll(two, 1, 1)
        return jnp.where(lane_of(one) % 2 == 0, one, two)

    def pack4(parts):
        total = parts[0]
        for k, part in enumerate(parts[1:], 1):
            total = jnp.where(lane_of(part) % 4 == (1 + k) % 4, pltpu.roll(part, k, 1), total)
        return total

    def lift_level2(v):
        c2, _, _ = lift_zero_extended(v, -4, nz + 3, True)
        o, _, _ = lift_zero_extended({k // 2: w for k, w in c2.items()}, -3, 10)
        return [o[k] for k in (*range(8), 8, 9, 10, -3, -2, -1)]

    def lift_level3(v):
        c2, _, _ = lift_zero_extended(v, -4, nz + 3, True)
        c3, _, _ = lift_zero_extended({k // 2: w for k, w in c2.items()}, -6, 12, True)
        o, _, _ = lift_zero_extended({k // 2: w for k, w in c3.items()}, -6, 10)
        return [o[k] for k in (*range(4), 4, 5, 6, 7, -4, -3, -2, -1, 8, 9, -6, -5)]

    def shift(v, k):
        return pltpu.roll(v, 128 - k, 1) if k else v

    def lift_level1(v):
        o, d1, s1 = lift_zero_extended(v, 0, nz - 1)
        return o, ((d1[nz // 2 - 1], s1[nz // 2 - 1]), (v[0], v[0] + BETA * d1[0]))

    def expand(h, lanes):
        hi, lo = halo_parts(h)
        return dot(jnp.concatenate([hi, lo, hi], axis=0), ra[:, lanes], ((0,), (0,)))

    level1, deeper = slice(0, 128), slice(128, 256)

    with jax.named_scope("load"):
        loads[0].wait()

    with jax.named_scope("ymsg"):
        for k, load in enumerate(x_loads):
            load.wait()
            hi, lo = halo_parts(x[CHUNK * k : CHUNK * k + CHUNK].reshape(CHUNK * nx, ny))
            first = dot(sa[...], hi, ((1,), (1,)))
            message = first[0:16] + first[16:32] + dot(sa[0:16], lo, ((1,), (1,)))
            for z in range(CHUNK):
                for c in range(2):
                    ys[c, CHUNK * k + z] = message[8 * c : 8 * c + 8, z * nx : (z + 1) * nx]
    with jax.named_scope("barw"):
        for tile in range(16):
            rows = slice(8 * tile, 8 * tile + 8)
            v = {k: x[k, rows] for k in (0, 1, 2, nz - 4, nz - 3, nz - 2, nz - 1)}
            last = v[nz - 1] + ALPHA * v[nz - 2]
            zs[0, 0, rows] = last
            zs[0, 1, rows] = v[nz - 2] + BETA * (v[nz - 3] + ALPHA * (v[nz - 4] + v[nz - 2]) + last)
            zs[1, 0, rows] = v[0]
            zs[1, 1, rows] = v[0] + BETA * (v[1] + ALPHA * (v[0] + v[2]))
        pl.semaphore_wait(barrier, len(TARGETS))
        y_copies = [send(ys.at[k], yr.at[k], (0, 0, c)) for k, c in enumerate(SIDES)]
        z_copies = [send(zs.at[a], zr.at[a], (s, 0, 0)) for a, s in enumerate(SIDES)]

    def hello(first, directions):
        for k, offsets in enumerate(directions):
            pl.semaphore_signal(
                hello_sem.at[first + k], inc=1, device_id=neighbour(offsets), device_id_type=pl.DeviceIdType.MESH
            )

    hello(0, [(a, 0, 0) for a in SIDES])

    with jax.named_scope("ycent"):
        for load in loads[1:]:
            load.wait()
        for z in range(nz):
            hi, lo = halo_parts(x[z])
            yc[z] = dot(jnp.concatenate([hi, lo], axis=1), wa[...]) + dot(hi, wb[...])
    with jax.named_scope("x2"):
        for z in range(nz):
            hi, lo = halo_parts(yc[z, :, deeper])
            q = dot(g2a[...], jnp.concatenate([hi, lo], axis=0)) + dot(g2b[...], hi)
            qs[z] = q

    with jax.named_scope("z23"):
        for tile in range(16):
            rows = slice(8 * tile, 8 * tile + 8)
            planes, lift = (PLANES2, lift_level2) if tile < 10 else (PLANES3, lift_level3)
            for k, v in zip(planes, lift({k: qs[k, rows] for k in range(nz)})):
                w[k, rows] = v

    for k in range(2):
        pl.semaphore_wait(hello_sem.at[k], 1)
    hello(2, [(0, b, 0) for b in SIDES])
    with jax.named_scope("x1"):
        for z in range(nz):
            hi, lo = halo_parts(yc[z, :, level1])
            q1[z] = dot(g1a[...], jnp.concatenate([hi, lo], axis=0)) + dot(g1b[...], hi)
    with jax.named_scope("z1"):
        for tile in range(17):
            rows = slice(8 * tile, 8 * tile + 8)
            o, pairs = lift_level1({k: q1[k, rows] for k in range(nz)})
            for k in range(nz):
                if tile < 16:
                    out[k, rows] = o[k]
                else:
                    xc[k] = o[k]
            if tile == 16:
                for a in range(2):
                    for r in range(2):
                        ec[a, r] = pairs[a][r]

    with jax.named_scope("ywait"):
        for copy in y_copies:
            copy.wait_recv()

    with jax.named_scope("halo"):
        h = jnp.concatenate([yr[0], yr[1]], axis=1).reshape(nz * 16, nx)
        hi, lo = halo_parts(h)
        both = jnp.concatenate([hi, lo], axis=1)
        rhs = ((1,), (1,))
        t2 = (dot(both, g2a[...], rhs) + dot(hi, g2b[...], rhs)).reshape(nz, 16, 128)
        from2 = dict(zip(PLANES2, lift_level2({k: t2[k] for k in range(nz)})))
        from3 = dict(zip(PLANES3, lift_level3({k: t2[k] for k in range(nz)})))
        level2_rows = lax.broadcasted_iota(jnp.int32, (16, 128), 1) < 80

    def halo_share(k):
        if k in from2 and k in from3:
            h = jnp.where(level2_rows, from2[k], from3[k])
        elif k in from2:
            h = jnp.where(level2_rows, from2[k], 0.0)
        else:
            h = jnp.where(level2_rows, 0.0, from3[k])
        return expand(h, deeper)

    with jax.named_scope("zplanes"):
        for k in range(8, 20):
            w[k] += halo_share(k)

    with jax.named_scope("zpack"):
        for a in range(2):
            near = [w.at[8 + 4 * a + k] for k in range(4)]
            ps[a, 0:64] = pack2(near[0][0:64], near[1][0:64])
            odd = [pack2(near[k][80:112], pltpu.roll(near[k + 1][80:112], 1, 1)) for k in (0, 2)]
            odd = [jnp.where(lane_of(v) % 4 == 3, v, near[2 * k][80:112]) for k, v in enumerate(odd)]
            third = near[2][0:64]
            ps[a, 64:128] = jnp.where(lane_of(third) % 2 == 0, third, jnp.concatenate(odd, axis=0))
            far = [w.at[16 + 2 * a + k] for k in range(2)]
            ds[a] = pack4([far[0][80:96], far[1][80:96], far[0][96:112], far[1][96:112]])
        for a, s in enumerate(SIDES):
            d_copy[a] = send(ds.at[a], dr.at[a], (2 * s, 0, 0))
        for a, s in enumerate(SIDES):
            p_copy[a] = send(ps.at[a], pr.at[a], (s, 0, 0))

    with jax.named_scope("halo1"):
        t1 = (dot(both, g1a[...], rhs) + dot(hi, g1b[...], rhs)).reshape(nz, 16, 136)
        t1, t1_pairs = lift_level1({k: t1[k] for k in range(nz)})
        for a in range(2):
            (one, two), (three, four) = ((t[0:8, 0:nx], t[8:16, 0:nx]) for t in t1_pairs[a])
            second, fourth = jnp.where(row < 2, one, pltpu.roll(two, 2, 0)), jnp.where(row < 2, three, pltpu.roll(four, 2, 0))
            ts[a] = jnp.where(row < 4, second, pltpu.roll(fourth, 4, 0))
        edge1 = [[ec[a, r] + expand(t1_pairs[a][r][:, nx : nx + 8], level1) for r in range(2)] for a in range(2)]
        for a, s in enumerate(SIDES):
            near, far = [w.at[8 + 4 * a + k] for k in range(4)], [w.at[16 + 2 * a + k] for k in range(2)]
            near3 = pack4([v[112:120] for v in near])
            far3 = pack4([far[0][112:120], far[1][112:120], far[0][112:120], far[1][112:120]])
            for b in range(2):
                e = 2 * a + b
                es[e, 0] = jnp.where(row < 4, slots(edge1[a], 2, 2 * b), pltpu.roll(near3, 4, 0) if b == 0 else near3)
                es[e, 1] = slots([pack2(near[0][64:72], near[1][64:72]), pack2(near[2][64:72], None)], 4, 4 * b)
                cs[e] = slots([far3], 4, 4 * b)
        for k in (2, 3):
            pl.semaphore_wait(hello_sem.at[k], 1)
        for a, s in enumerate(SIDES):
            for b, t in enumerate(SIDES):
                c_copy[2 * a + b] = send(cs.at[2 * a + b], cr.at[2 * a + b], (2 * s, t, 0))
        for a, s in enumerate(SIDES):
            t_copy[a] = send(ts.at[a], tr.at[a], (s, 0, 0))
            for b, t in enumerate(SIDES):
                e_copy[2 * a + b] = send(es.at[2 * a + b], er.at[2 * a + b], (s, t, 0))

    with jax.named_scope("xs"):
        full = [xc[k] + expand(t1[k][:, nx : nx + 8], level1) for k in range(nz)]
        for k in range(nz // 4):
            for b in range(2):
                xs[b, k] = slots(full[4 * k : 4 * k + 4], 2, 2 * b)
        pairs2, thirds = [], []
        for k in range(0, 8, 2):
            one, two = w[k] + halo_share(k), w[k + 1] + halo_share(k + 1)
            f2[k], f2[k + 1] = one[0:64], two[0:64]
            pairs2.append(pack2(one[64:72], two[64:72]))
            if k < 4:
                f3[k], f3[k + 1] = one[80:112], two[80:112]
                thirds += [one[112:120], two[112:120]]
        for b, t in enumerate(SIDES):
            for k in range(2):
                xs[b, 4 + k] = slots(pairs2[2 * k : 2 * k + 2], 4, 4 * b)
            xs[b, 6] = slots([pack4(thirds)], 4, 4 * b)
            x_copy[b] = send(xs.at[b], xr.at[b], (0, t, 0))

    with jax.named_scope("zwait"):
        for copy in z_copies:
            copy.wait_recv()

    with jax.named_scope("own1"):
        for k in range(nz):
            out[k] += expand(t1[k][:, 0:nx], level1)

    with jax.named_scope("zraw"):
        for a in range(2):
            for r in range(2):
                hi, lo = halo_parts(zr[a, r])
                y = dot(jnp.concatenate([hi, lo], axis=1), wa[:, level1]) + dot(hi, wb[:, level1])
                hi, lo = halo_parts(y)
                zr[a, r] = dot(g1a[0:nx], jnp.concatenate([hi, lo], axis=0)) + dot(g1b[0:nx], hi)

    def take_far(a, rows, v, first):
        one, two = shift(v, first), shift(v, first + 1)
        if a == 0:
            f3[0, rows] += one
            f3[1, rows] += two
            f3[2, rows] += float(far_share[0]) * one + float(far_share[1]) * two
        else:
            f3[2, rows] += one
            f3[3, rows] += two

    ends = ((0, 0, 0), (nx - 8, nx // 2 - 8, nx // 4 - 8))
    with jax.named_scope("wait_t"):
        for a in range(2):
            t_copy[a].wait_recv()
            for r in range(2):
                quad = pltpu.roll(tr[a], 4, 0) if r else tr[a]
                quad = [jnp.where(row < 2, pltpu.roll(quad, 6, 0) if c else quad, 0.0) for c in range(2)]
                zr[a, r] += expand(jnp.concatenate(quad, axis=0), level1)

    with jax.named_scope("wait_x"):
        for b, (r1, r2, r3) in enumerate(ends):
            x_copy[b].wait_recv()
            for k in range(16):
                out[k, r1 : r1 + 8] += spread(0, b, xr[b, k // 4], 2 * (k % 4))
            for k in range(4):
                pair = spread(1, b, xr[b, 4 + k // 2], 4 * (k % 2))
                for q in range(2):
                    f2[2 * k + q, r2 : r2 + 8] += shift(pair, q)
            quad = spread(2, b, xr[b, 6], 0)
            for k in range(4):
                f3[k, r3 : r3 + 8] += shift(quad, k)

    with jax.named_scope("wait_z"):
        for group in (d_copy, c_copy, e_copy, p_copy):
            for copy in group.values():
                copy.wait_recv()
    with jax.named_scope("edges"):
        for a in range(2):
            for half in range(2):
                take_far(a, slice(16 * half, 16 * half + 16), dr[a], 2 * half)
                for q in range(2):
                    f3[2 * half + q] += shift(pr[a, 64 + 32 * half : 96 + 32 * half], 2 * q)
            for b, (r1, r2, r3) in enumerate(ends):
                e = 2 * a + b
                for r in range(2):
                    zr[a, r, r1 : r1 + 8] += spread(0, b, er[e, 0], 2 * r)
                    pr[a, 64 * r + r2 : 64 * r + r2 + 8] += spread(1, b, er[e, 1], 4 * r)
                quad = spread(2, b, er[e, 0], 4)
                for j in range(4):
                    f3[j, r3 : r3 + 8] += shift(quad, j)
                take_far(a, slice(r3, r3 + 8), spread(2, b, cr[e], 0), 0)

    with jax.named_scope("zfaces"):
        for tile in range(16):
            rows = slice(8 * tile, 8 * tile + 8)
            one, two = zr[0, 0, rows], zr[0, 1, rows]
            s10 = BETA * one
            d2m = one + GAMMA * (two + s10)
            d20 = GAMMA * s10
            s20 = s10 + DELTA * (d2m + d20)
            out[0, rows] += ZETA * s20
            out[1, rows] += (1 / ZETA) * d20
            out[2, rows] += (ZETA * DELTA) * d20
            one, two = zr[1, 0, rows], zr[1, 1, rows]
            d17 = ALPHA * one
            s17 = BETA * d17
            d27 = d17 + GAMMA * (s17 + two + s17)
            d26 = GAMMA * s17
            s27 = s17 + DELTA * (d26 + d27)
            out[nz - 4, rows] += (ZETA * DELTA) * d26
            out[nz - 3, rows] += (1 / ZETA) * d26
            out[nz - 2, rows] += ZETA * s27
            out[nz - 1, rows] += (1 / ZETA) * d27

    with jax.named_scope("final"):
        lane3 = lax.broadcasted_iota(jnp.int32, (32, 128), 1)
        lane2 = lax.broadcasted_iota(jnp.int32, (64, 128), 1)
        parts = []
        for a in range(2):
            first, second = pr[a, 0:64], pr[a, 64:128]
            parts.append((first, shift(first, 1), second))
        for k in range(8):
            total = f2[k]
            for a in range(2):
                total = add((1, total), *[(float(shares[a][k, r]), parts[a][r]) for r in range(3) if abs(shares[a][k, r]) > 1e-12])
            f2[k] = total
            if k % 2 == 0:
                j = k // 2
                even = pl.ds(0, 32, 2)
                f2[k, even, :] = jnp.where(lane3 % 4 == 0, shift(f3[j], 1), f2[k, even, :])
            even = pl.ds(0, 64, 2)
            out[2 * k, even, :] = jnp.where(lane2 % 2 == 0, f2[k], out[2 * k, even, :])

    with jax.named_scope("sendwait"):
        for copy in copies:
            copy.wait_send()


def local(turbulence, consts, edge_shares, shares, far_share):
    nz, nx, ny = turbulence.shape
    f32 = jnp.float32
    vmem = lambda *shape: pltpu.VMEM(shape, f32)
    pair = lambda *shape: [vmem(*shape), vmem(*shape)]
    count = 20
    return pl.pallas_call(
        functools.partial(kernel, edge_shares, shares, far_share),
        out_shape=jax.ShapeDtypeStruct(turbulence.shape, f32),
        in_specs=[pl.BlockSpec(memory_space=pltpu.HBM)] * (1 + len(consts)),
        out_specs=pl.BlockSpec(memory_space=pltpu.VMEM),
        scratch_shapes=[
            vmem(nz, nx, ny),
            *[pltpu.VMEM(c.shape, c.dtype) for c in consts],
            vmem(nz, nx, 2 * ny), vmem(nz, 136, ny), vmem(nz, 128, ny), vmem(20, 128, ny),
            vmem(8, 64, ny), vmem(4, 32, ny),
            vmem(nz, 8, ny), vmem(2, 2, 8, ny),
            *pair(2, nz, 8, nx),
            *pair(2, 7, 8, ny),
            *pair(2, 2, nx, ny),
            *pair(2, 8, nx),
            *pair(2, 128, ny),
            *pair(4, 2, 8, ny),
            *pair(2, 16, ny),
            *pair(4, 8, ny),
            pltpu.SemaphoreType.DMA((nz // CHUNK + len(consts),)),
            pltpu.SemaphoreType.DMA((count,)),
            pltpu.SemaphoreType.DMA((count,)),
            pltpu.SemaphoreType.REGULAR((4,)),
        ],
        compiler_params=pltpu.CompilerParams(collective_id=0, has_side_effects=True, vmem_limit_bytes=48 << 20),
    )(*[pltpu.with_memory_space_constraint(a, pltpu.HBM) for a in (turbulence, *consts)])


def solution(mesh):
    def run(turbulence):
        nz, n, _ = turbulence.shape
        t = tables(n, n * lax.axis_size("gx"))
        names = ("sa", "wa", "wb", "g1a", "g1b", "g2a", "g2b", "ra")
        along_x, along_z = (n, n * lax.axis_size("gx")), (nz, nz * lax.axis_size("gz"))
        consts = [jnp.asarray(t[k]) for k in names]
        return local(turbulence, consts, x_shares(*along_x), level2_shares(*along_z), level3_shares(*along_z))

    spec = P(*AXES)
    return jax.shard_map(run, mesh=mesh, in_specs=(spec,), out_specs=spec, check_vma=False)
```
